512 devices in a mesh: track: 8 (over y_hi, x), tm: 64 (over z, y_lo, core).
Axes of the slice: x: 4, y: 4 (y_hi: 2, y_lo: 2; y = y_hi * 2 + y_lo), z: 16, core: 2. Of those that a mesh axis runs over, the one named last changes fastest.
Arguments:
- time_query: bfloat16 [2, 4096, 8, 1024], P(None, 'tm', 'track'), may hold values from -6 to 6
- time_memory: bfloat16 [2, 4096, 8, 256], P(None, 'tm', 'track'), may hold values from -6 to 6
- time_grad_out: bfloat16 [2, 4096, 8, 1024], P(None, 'tm', 'track'), may hold values from -6 to 6
- track_query: bfloat16 [2, 4096, 8, 1024], P(None, 'tm', 'track'), may hold values from -6 to 6
- track_memory: bfloat16 [2, 4096, 8, 256], P(None, 'tm', 'track'), may hold values from -6 to 6
- track_grad_out: bfloat16 [2, 4096, 8, 1024], P(None, 'tm', 'track'), may hold values from -6 to 6
Outputs:
- time_query_grad: bfloat16 [2, 4096, 8, 1024], P(None, 'tm', 'track')
- time_memory_grad: bfloat16 [2, 4096, 8, 256], P(None, 'tm', 'track')
- track_query_grad: bfloat16 [2, 4096, 8, 1024], P(None, 'tm', 'track')
- track_memory_grad: bfloat16 [2, 4096, 8, 256], P(None, 'tm', 'track')
The draws below stay inside these ranges and needn't reach their ends.
All inputs are finite; a program needn't handle non-finite values.
Results may differ from the reference program's by a relative error of at most 0.017.
Values may be sent and summed in bfloat16 or wider, within the bound.
No kernel may reach another device: no remote copies, remote signals or barrier semaphores. Data moves between devices by JAX's collectives and lax.ppermute only.
A program may use at most 64 MiB of HBM per device.

```python
import math
import jax
import jax.numpy as jnp
from jax import lax

SONGS = 2
HEAD = 128
TIME_HEADS = 8
TRACK_HEADS = 8
LENGTH = 4096
TRACKS = 8


def row_scaled(key, values, low, high):
    factor = jnp.exp(jax.random.uniform(key, values.shape[:-1] + (1,), jnp.float32, math.log(low), math.log(high)))
    return jnp.clip(values * factor, -6.0, 6.0)


def draw_time_query(key, part):
    key = jax.random.fold_in(key, 11)
    first, second = jax.random.split(key)
    shape = (SONGS, LENGTH, TRACKS, TIME_HEADS * HEAD)
    values = row_scaled(second, jax.random.normal(first, shape, jnp.float32), 0.25, 2.5)
    return values.astype(jnp.bfloat16)


def draw_time_memory(key, part):
    key = jax.random.fold_in(key, 12)
    first, second, third = jax.random.split(key, 3)
    shape = (SONGS, LENGTH, TRACKS, HEAD)
    keys = row_scaled(second, jax.random.normal(first, shape, jnp.float32), 0.3, 3.0)
    values = jnp.clip(jax.random.normal(third, shape, jnp.float32), -6.0, 6.0)
    return jnp.concatenate([keys, values], axis=-1).astype(jnp.bfloat16)


def draw_track_query(key, part):
    key = jax.random.fold_in(key, 13)
    first, second = jax.random.split(key)
    shape = (SONGS, LENGTH, TRACKS, TRACK_HEADS * HEAD)
    values = row_scaled(second, jax.random.normal(first, shape, jnp.float32), 0.25, 2.5)
    return values.astype(jnp.bfloat16)


def draw_track_memory(key, part):
    key = jax.random.fold_in(key, 14)
    first, second, third = jax.random.split(key, 3)
    shape = (SONGS, LENGTH, TRACKS, HEAD)
    keys = row_scaled(second, jax.random.normal(first, shape, jnp.float32), 0.3, 3.0)
    values = jnp.clip(jax.random.normal(third, shape, jnp.float32), -6.0, 6.0)
    return jnp.concatenate([keys, values], axis=-1).astype(jnp.bfloat16)


def levels(key, dims, cuts, least, high):
    def one(axis_at, shards_of):
        heights = jax.random.uniform(jax.random.fold_in(jax.random.fold_in(key, 6), axis_at), (shards_of,), jnp.float32, least / len(cuts), high / len(cuts))
        return jnp.repeat(jnp.exp(heights), dims[axis_at] // shards_of).reshape((-1,) + (1,) * (len(dims) - axis_at - 1))

    level = one(*cuts[0])
    for cut in cuts[1:]:
        level = level * one(*cut)
    return level


def scatter_about(stream_key, shape, spread, most, shards=(), kind=jnp.bfloat16):
    array = spread * jax.random.normal(stream_key, shape, jnp.float32)
    if shards:
        array = array * levels(stream_key, shape, shards, -0.22, 0.18)
    return jnp.clip(array, -most, most).astype(kind)


def setup_inputs(seed: int = 0) -> dict:
    seeds = jax.random.split(jax.random.key(seed), 7)
    time_query = draw_time_query(jax.random.fold_in(seeds[6], 71), 0)
    time_memory = draw_time_memory(jax.random.fold_in(seeds[6], 71), 0)
    time_grad_out = scatter_about(seeds[2], (SONGS, LENGTH, TRACKS, TIME_HEADS * HEAD), 1.0, 6.0, ((1, 64), (2, 8)))
    track_query = draw_track_query(jax.random.fold_in(seeds[6], 71), 0)
    track_memory = draw_track_memory(jax.random.fold_in(seeds[6], 71), 0)
    track_grad_out = scatter_about(seeds[5], (SONGS, LENGTH, TRACKS, TRACK_HEADS * HEAD), 1.0, 6.0, ((1, 64), (2, 8)))
    return dict(time_query=time_query, time_memory=time_memory, time_grad_out=time_grad_out, track_query=track_query, track_memory=track_memory, track_grad_out=track_grad_out)


def round_trip(values):
    return lax.optimization_barrier(values.astype(jnp.bfloat16)).astype(jnp.float32)


def time_track(query, memory, grad_out):
    length = query.shape[0]
    scale = HEAD ** -0.5
    width = math.gcd(length, 512)
    keys = memory[:, :HEAD]
    values = memory[:, HEAD:]
    key_grad = jnp.zeros((length, HEAD), jnp.float32)
    value_grad = jnp.zeros((length, HEAD), jnp.float32)
    pieces = []
    for block in range(length // width):
        begin = block * width
        end = begin + width
        rows = query[begin:end].reshape(width * TIME_HEADS, HEAD)
        grads = grad_out[begin:end].reshape(width * TIME_HEADS, HEAD)
        positions = begin + jnp.arange(width * TIME_HEADS, dtype=jnp.int32) // TIME_HEADS
        mask = jnp.arange(end, dtype=jnp.int32)[None, :] <= positions[:, None]
        scores = jnp.dot(rows, keys[:end].T, preferred_element_type=jnp.float32) * scale
        scores = jnp.where(mask, scores, -jnp.inf)
        top = jnp.max(scores, axis=1, keepdims=True)
        log_total = top + jnp.log(jnp.sum(jnp.exp(scores - top), axis=1, keepdims=True))
        weights = jnp.exp(scores - log_total)
        products = jnp.dot(grads, values[:end].T, preferred_element_type=jnp.float32)
        delta = jnp.sum(weights * products, axis=1, keepdims=True)
        slopes = weights * (products - delta)
        weights_half = weights.astype(jnp.bfloat16)
        slopes_half = slopes.astype(jnp.bfloat16)
        query_piece = jnp.dot(slopes_half, keys[:end], preferred_element_type=jnp.float32) * scale
        pieces.append(query_piece.reshape(width, TIME_HEADS * HEAD))
        key_grad = key_grad.at[:end].add(jnp.dot(slopes_half.T, rows, preferred_element_type=jnp.float32) * scale)
        value_grad = value_grad.at[:end].add(jnp.dot(weights_half.T, grads, preferred_element_type=jnp.float32))
    query_grad = jnp.concatenate(pieces, axis=0).astype(jnp.bfloat16)
    memory_grad = jnp.concatenate([key_grad, value_grad], axis=1).astype(jnp.bfloat16)
    return query_grad, memory_grad


def track_part(track_query, track_memory, track_grad_out):
    scale = HEAD ** -0.5
    shaped = (SONGS, LENGTH, TRACKS, TRACK_HEADS, HEAD)
    query = track_query.reshape(shaped).astype(jnp.float32)
    grad_out = track_grad_out.reshape(shaped).astype(jnp.float32)
    keys = track_memory[..., :HEAD].astype(jnp.float32)
    values = track_memory[..., HEAD:].astype(jnp.float32)
    scores = jnp.einsum("slqhd,sltd->slqht", query, keys) * scale
    top = jnp.max(scores, axis=-1, keepdims=True)
    log_total = top + jnp.log(jnp.sum(jnp.exp(scores - top), axis=-1, keepdims=True))
    weights = jnp.exp(scores - log_total)
    products = jnp.einsum("slqhd,sltd->slqht", grad_out, values)
    delta = jnp.sum(weights * products, axis=-1, keepdims=True)
    slopes = weights * (products - delta)
    weights_half = round_trip(weights)
    slopes_half = round_trip(slopes)
    query_grad = jnp.einsum("slqht,sltd->slqhd", slopes_half, keys) * scale
    key_grad = jnp.einsum("slqht,slqhd->sltd", slopes_half, query) * scale
    value_grad = jnp.einsum("slqht,slqhd->sltd", weights_half, grad_out)
    query_grad = query_grad.reshape(SONGS, LENGTH, TRACKS, TRACK_HEADS * HEAD).astype(jnp.bfloat16)
    memory_grad = jnp.concatenate([key_grad, value_grad], axis=-1).astype(jnp.bfloat16)
    return query_grad, memory_grad


def reference(time_query, time_memory, time_grad_out, track_query, track_memory, track_grad_out):
    def flatten(values):
        return jnp.transpose(values, (0, 2, 1, 3)).reshape(SONGS * TRACKS, LENGTH, values.shape[3])

    def unflatten(values):
        return jnp.transpose(values.reshape(SONGS, TRACKS, LENGTH, values.shape[2]), (0, 2, 1, 3))

    results = lax.map(lambda item: time_track(item[0], item[1], item[2]),
                      (flatten(time_query), flatten(time_memory), flatten(time_grad_out)))
    time_query_grad = unflatten(results[0])
    time_memory_grad = unflatten(results[1])
    track_query_grad, track_memory_grad = track_part(track_query, track_memory, track_grad_out)
    return (time_query_grad, time_memory_grad, track_query_grad, track_memory_grad)
```

```python
import functools
import math

import jax
import jax.numpy as jnp
from jax import lax
from jax.experimental import pallas as pl
from jax.experimental.pallas import tpu as pltpu
from jax.sharding import Mesh, PartitionSpec as P

FAR_BELOW = -1e30
LOG2E = math.log2(math.e)
NT = (((1,), (1,)), ((), ()))
NN = (((1,), (0,)), ((), ()))
TN = (((0,), (0,)), ((), ()))
VMEM = pl.BlockSpec(memory_space=pltpu.VMEM)
SMEM = pl.BlockSpec(memory_space=pltpu.SMEM)
PARAMS = pltpu.CompilerParams(vmem_limit_bytes=48 * 1024 * 1024)


def dot(a, b, dims):
    return lax.dot_general(a, b, dims, preferred_element_type=jnp.float32)


def swapped(block, axis):
    return lax.ppermute(block, axis, [(0, 1), (1, 0)])


def fill_mask(info, mask, block, groups):
    low, side, core = info[1], info[2], info[3]
    half = block // 2

    def place(index):
        return lax.rem(index + core * half, block)

    key = lax.broadcasted_iota(jnp.int32, (block, block), 0)
    row = lax.broadcasted_iota(jnp.int32, (block, block), 1)
    causal = jnp.where(place(key) <= place(row), 0.0, FAR_BELOW)
    for g in range(groups):
        before = jnp.where(g < low, 0.0, FAR_BELOW)
        at = g == low
        own = jnp.where(at, causal, before)
        other = jnp.where(jnp.logical_and(at, side == 0), 0.0, before)
        mask[g * block : (g + 1) * block, :block] = own
        mask[g * block : (g + 1) * block, block:] = jnp.broadcast_to(other, (block, block))


def group_of(memory, index, head, part):
    pieces = [memory[g, index, :, part * head : (part + 1) * head] for g in range(memory.shape[0])]
    return jnp.concatenate(pieces, axis=0)


def head_rows(own, other, column, head):
    cut = slice(column * head, (column + 1) * head)
    return jnp.concatenate([own[:, cut], other[:, cut]], axis=0)


def stats_kernel(heads, head, factor, info, own, other, memory, out, mask, most, total, weighted):
    groups, _, block, _ = memory.shape
    fill_mask(info, mask, block, groups)
    most[...] = jnp.full(most.shape, FAR_BELOW, jnp.float32)
    total[...] = jnp.zeros(total.shape, jnp.float32)
    weighted[...] = jnp.zeros(weighted.shape, jnp.float32)

    def visit(index, masked):
        keys = group_of(memory, index, head, 0)
        values = group_of(memory, index, head, 1)
        for h in range(heads):
            scores = dot(keys, head_rows(own, other, h, head), NT)
            products = dot(values, head_rows(own, other, heads + h, head), NT)
            if masked:
                scores = scores + mask[...]
            rows = scores.shape[1]
            scores = scores.reshape(-1, 8, rows)
            products = products.reshape(-1, 8, rows)
            raised = jnp.maximum(most[h], jnp.max(scores, axis=0))
            fade = jnp.exp2((most[h] - raised) * factor)
            weights = jnp.exp2((scores - raised[None]) * factor)
            most[h] = raised
            total[h] = total[h] * fade + jnp.sum(weights, axis=0)
            weighted[h] = weighted[h] * fade + jnp.sum(weights * products, axis=0)

    visit(0, True)

    @pl.loop(1, info[0] + 1)
    def _(index):
        visit(index, False)

    for h in range(heads):
        top = jnp.max(most[h], axis=0, keepdims=True)
        fade = jnp.exp2((most[h] - top) * factor)
        out[0, h : h + 1] = top
        out[1, h : h + 1] = jnp.sum(total[h] * fade, axis=0, keepdims=True)
        out[2, h : h + 1] = jnp.sum(weighted[h] * fade, axis=0, keepdims=True)


def grads_kernel(
    heads, head, scale, info, own, other, memory, mine, theirs,
    own_grad, other_grad, memory_grad,
    mask, queries, grads, weights_half, slopes_half, query_grad, shift, delta,
):
    groups, _, block, _ = memory.shape
    rows = 2 * block
    factor = scale * LOG2E
    fill_mask(info, mask, block, groups)

    def turned(stat):
        return jnp.concatenate([theirs[stat, :, block:], theirs[stat, :, :block]], axis=1)

    most = [mine[0], turned(0)]
    top = jnp.maximum(most[0], most[1])
    fades = [jnp.exp2((m - top) * factor) for m in most]
    total = mine[1] * fades[0] + turned(1) * fades[1]
    weighted = mine[2] * fades[0] + turned(2) * fades[1]
    shift[...] = top * factor + jnp.log(total) * LOG2E
    delta[...] = weighted / total
    for h in range(heads):
        queries[h * rows : (h + 1) * rows] = head_rows(own, other, h, head)
        grads[h * rows : (h + 1) * rows] = head_rows(own, other, heads + h, head)
    query_grad[...] = jnp.zeros(query_grad.shape, jnp.float32)

    def visit(index, masked):
        keys = group_of(memory, index, head, 0)
        values = group_of(memory, index, head, 1)
        for h in range(heads):
            cut = slice(h * rows, (h + 1) * rows)
            scores = dot(keys, queries[cut], NT)
            products = dot(values, grads[cut], NT)
            if masked:
                scores = scores + mask[...]
            weights = jnp.exp2(scores * factor - shift[h : h + 1])
            slopes = weights * (products - delta[h : h + 1])
            weights_half[:, cut] = weights.astype(jnp.bfloat16)
            slopes_half[:, cut] = slopes.astype(jnp.bfloat16)
        value_grad = dot(weights_half[...], grads[...], NN).astype(jnp.bfloat16)
        key_grad = (dot(slopes_half[...], queries[...], NN) * scale).astype(jnp.bfloat16)
        for g in range(groups):
            cut = slice(g * block, (g + 1) * block)
            memory_grad[g, index, :, :head] = key_grad[cut]
            memory_grad[g, index, :, head:] = value_grad[cut]
        query_grad[...] += dot(keys, slopes_half[...], TN)

    visit(0, True)

    @pl.loop(1, info[0] + 1)
    def _(index):
        visit(index, False)

    for h in range(heads):
        piece = query_grad[:, h * rows : (h + 1) * rows].T * scale
        own_grad[:, h * head : (h + 1) * head] = piece[:block]
        other_grad[:, h * head : (h + 1) * head] = piece[block:].astype(jnp.bfloat16)


def track_kernel(heads, head, scale, span, queries, grads, memory, query_grad, memory_grad):
    tracks, positions, _ = memory.shape
    factor = scale * LOG2E
    key_place = lax.rem(lax.broadcasted_iota(jnp.int32, (tracks * span, heads * span), 0), span)
    row_place = lax.rem(lax.broadcasted_iota(jnp.int32, (tracks * span, heads * span), 1), span)
    mask = jnp.where(key_place == row_place, 0.0, FAR_BELOW)
    for begin in range(0, positions, span):
        at = slice(begin, begin + span)
        rows = jnp.concatenate([queries[at, h * head : (h + 1) * head] for h in range(heads)], axis=0)
        out_rows = jnp.concatenate([grads[at, h * head : (h + 1) * head] for h in range(heads)], axis=0)
        keys = jnp.concatenate([memory[t, at, :head] for t in range(tracks)], axis=0)
        values = jnp.concatenate([memory[t, at, head:] for t in range(tracks)], axis=0)
        scores = dot(keys, rows, NT) + mask
        products = dot(values, out_rows, NT)
        top = jnp.max(scores, axis=0, keepdims=True)
        raw = jnp.exp2((scores - top) * factor)
        inverse = 1.0 / jnp.sum(raw, axis=0, keepdims=True)
        weights = raw * inverse
        delta = jnp.sum(weights * products, axis=0, keepdims=True)
        slopes = weights * (products - delta)
        weights_half = weights.astype(jnp.bfloat16)
        slopes_half = slopes.astype(jnp.bfloat16)
        value_grad = dot(weights_half, out_rows, NN).astype(jnp.bfloat16)
        key_grad = (dot(slopes_half, rows, NN) * scale).astype(jnp.bfloat16)
        row_grad = (dot(keys, slopes_half, TN).T * scale).astype(jnp.bfloat16)
        for t in range(tracks):
            cut = slice(t * span, (t + 1) * span)
            memory_grad[t, at, :head] = key_grad[cut]
            memory_grad[t, at, head:] = value_grad[cut]
        for h in range(heads):
            query_grad[at, h * head : (h + 1) * head] = row_grad[h * span : (h + 1) * span]


def body(time_query, time_memory, time_grad_out, track_query, track_memory, track_grad_out):
    songs, pos_dev, _, feature = time_query.shape
    head = time_memory.shape[3] // 2
    heads = feature // head
    scale = head ** (-0.5)
    block = 2 * pos_dev
    rows = 2 * block
    core = lax.axis_index("core")
    side = lax.axis_index("side")
    low = lax.axis_index("low")
    high = lax.axis_index("high")
    n_low = lax.axis_size("low")
    n_high = lax.axis_size("high")
    tracks = lax.axis_size("track")
    info = jnp.stack([high, low, side, core]).astype(jnp.int32)

    def of_song(array, index):
        return lax.dynamic_index_in_dim(array, index, 0, keepdims=False)

    memory = time_memory[:, :, 0]
    with jax.named_scope("memory_songs"):
        memory = jnp.concatenate(
            [of_song(memory, core), swapped(of_song(memory, 1 - core), "core")], axis=0
        )
    with jax.named_scope("memory_high"):
        held = [memory]
        for s in range(1, n_high):
            held.append(lax.ppermute(memory, "high", [(i, i + s) for i in range(n_high - s)]))
        held = jnp.stack(held)
    with jax.named_scope("memory_low"):
        held = lax.all_to_all(
            jnp.broadcast_to(held[None], (n_low, *held.shape)), "low", 0, 0, tiled=True
        )
    with jax.named_scope("query_songs"):
        packed = jnp.concatenate([time_query[:, :, 0], time_grad_out[:, :, 0]], axis=2)
        own = jnp.concatenate(
            [of_song(packed, core), swapped(of_song(packed, 1 - core), "core")], axis=0
        )
    with jax.named_scope("query_sides"):
        other = swapped(own, "side")

    with jax.named_scope("track_gather"):
        track_blocks = track_memory.reshape(1, block, 2 * head)
        everything = lax.all_to_all(
            jnp.broadcast_to(track_blocks, (tracks, block, 2 * head)), "track", 0, 0, tiled=True
        )
    track_query_grad, track_partial = pl.pallas_call(
        functools.partial(track_kernel, heads, head, scale, 32),
        out_shape=(
            jax.ShapeDtypeStruct((block, feature), jnp.bfloat16),
            jax.ShapeDtypeStruct((tracks, block, 2 * head), jnp.bfloat16),
        ),
        in_specs=[VMEM] * 3,
        out_specs=(VMEM, VMEM),
        compiler_params=PARAMS,
        name="track_core",
    )(track_query.reshape(block, feature), track_grad_out.reshape(block, feature), everything)

    mine = pl.pallas_call(
        functools.partial(stats_kernel, heads, head, scale * LOG2E),
        out_shape=jax.ShapeDtypeStruct((3, heads, rows), jnp.float32),
        in_specs=[SMEM] + [VMEM] * 3,
        out_specs=VMEM,
        scratch_shapes=[pltpu.VMEM((n_low * block, rows), jnp.float32)]
        + [pltpu.VMEM((heads, 8, rows), jnp.float32)] * 3,
        compiler_params=PARAMS,
        name="time_stats",
    )(info, own, other, held)
    with jax.named_scope("stats_sides"):
        theirs = swapped(mine, "side")
    own_grad, other_grad, memory_grad = pl.pallas_call(
        functools.partial(grads_kernel, heads, head, scale),
        out_shape=(
            jax.ShapeDtypeStruct((block, feature), jnp.float32),
            jax.ShapeDtypeStruct((block, feature), jnp.bfloat16),
            jax.ShapeDtypeStruct((n_low, n_high, block, 2 * head), jnp.bfloat16),
        ),
        in_specs=[SMEM] + [VMEM] * 5,
        out_specs=(VMEM, VMEM, VMEM),
        scratch_shapes=[
            pltpu.VMEM((n_low * block, rows), jnp.float32),
            pltpu.VMEM((heads * rows, head), jnp.bfloat16),
            pltpu.VMEM((heads * rows, head), jnp.bfloat16),
            pltpu.VMEM((n_low * block, heads * rows), jnp.bfloat16),
            pltpu.VMEM((n_low * block, heads * rows), jnp.bfloat16),
            pltpu.VMEM((head, heads * rows), jnp.float32),
            pltpu.VMEM((heads, rows), jnp.float32),
            pltpu.VMEM((heads, rows), jnp.float32),
        ],
        compiler_params=PARAMS,
        name="time_grads",
    )(info, own, other, held, mine, theirs)

    with jax.named_scope("memory_grad_low"):
        parts = lax.all_to_all(memory_grad, "low", 0, 0, tiled=True)
        sums = jnp.sum(parts.astype(jnp.float32), axis=0)
    with jax.named_scope("memory_grad_high"):
        gathered = sums[0]
        for s in range(1, n_high):
            back = lax.ppermute(
                sums[s].astype(jnp.bfloat16), "high", [(i + s, i) for i in range(n_high - s)]
            )
            gathered = gathered + back.astype(jnp.float32)
        gathered = gathered.astype(jnp.bfloat16)

    def to_songs(array):
        ours = array[:pos_dev]
        back = swapped(array[pos_dev:], "core")
        first = jnp.where(core == 0, ours, back)
        second = jnp.where(core == 0, back, ours)
        return jnp.stack([first, second])[:, :, None, :]

    with jax.named_scope("memory_grad_songs"):
        time_memory_grad = to_songs(gathered)
    with jax.named_scope("query_grad_sides"):
        query_grad = own_grad + swapped(other_grad, "side").astype(jnp.float32)
    with jax.named_scope("query_grad_songs"):
        time_query_grad = to_songs(query_grad.astype(jnp.bfloat16))
    with jax.named_scope("track_scatter"):
        track_parts = lax.all_to_all(track_partial, "track", 0, 0, tiled=True)
        track_memory_grad = jnp.sum(track_parts.astype(jnp.float32), axis=0).astype(jnp.bfloat16)
    return (
        time_query_grad,
        time_memory_grad,
        track_query_grad.reshape(track_query.shape),
        track_memory_grad.reshape(track_memory.shape),
    )


def solution(mesh):
    tracks, times = mesh.devices.shape
    chips = times // 4
    high = next(n for n in (4, 2, 1) if chips % n == 0)
    axes = ("track", "high", "low", "side", "core")
    finer = Mesh(mesh.devices.reshape(tracks, high, chips // high, 2, 2), axes)
    placed = P(None, axes[1:], "track", None)
    return jax.shard_map(
        body,
        mesh=finer,
        in_specs=(placed,) * 6,
        out_specs=(placed,) * 4,
        check_vma=False,
    )
```

```python
import functools
import math

import jax
import jax.numpy as jnp
from jax import lax
from jax.experimental import pallas as pl
from jax.experimental.pallas import tpu as pltpu
from jax.sharding import Mesh, PartitionSpec as P

FAR_BELOW = -1e30
LOG2E = math.log2(math.e)
NT = (((1,), (1,)), ((), ()))
NN = (((1,), (0,)), ((), ()))
TN = (((0,), (0,)), ((), ()))
VMEM = pl.BlockSpec(memory_space=pltpu.VMEM)
SMEM = pl.BlockSpec(memory_space=pltpu.SMEM)
PARAMS = pltpu.CompilerParams(vmem_limit_bytes=48 * 1024 * 1024)


def dot(a, b, dims):
    return lax.dot_general(a, b, dims, preferred_element_type=jnp.float32)


def after(block, earlier):
    return lax.optimization_barrier((block, earlier))[0]


def swapped(block, axis):
    return lax.ppermute(block, axis, [(0, 1), (1, 0)])


def fill_mask(info, mask, block, groups):
    low, side, core = info[1], info[2], info[3]
    half = block // 2

    def place(index):
        return lax.rem(index + core * half, block)

    key = lax.broadcasted_iota(jnp.int32, (block, block), 0)
    row = lax.broadcasted_iota(jnp.int32, (block, block), 1)
    causal = jnp.where(key <= place(row), 0.0, FAR_BELOW)
    for g in range(groups):
        before = jnp.where(g < low, 0.0, FAR_BELOW)
        at = g == low
        own = jnp.where(at, causal, before)
        other = jnp.where(jnp.logical_and(at, side == 0), 0.0, before)
        mask[g * block : (g + 1) * block, :block] = own
        mask[g * block : (g + 1) * block, block:] = jnp.broadcast_to(other, (block, block))


def group_of(memory, index, head, part):
    pieces = [memory[g, index, :, part * head : (part + 1) * head] for g in range(memory.shape[0])]
    return jnp.concatenate(pieces, axis=0)


def head_rows(own, other, column, head):
    cut = slice(column * head, (column + 1) * head)
    return jnp.concatenate([own[:, cut], other[:, cut]], axis=0)


def stats_kernel(heads, head, factor, info, own, other, memory, out, mask, most, total, weighted):
    groups, block = memory.shape[0] // 2, 2 * memory.shape[2]
    fill_mask(info, mask, block, groups)
    most[...] = jnp.full(most.shape, FAR_BELOW, jnp.float32)
    total[...] = jnp.zeros(total.shape, jnp.float32)
    weighted[...] = jnp.zeros(weighted.shape, jnp.float32)

    def visit(index, masked):
        keys = group_of(memory, index, head, 0)
        values = group_of(memory, index, head, 1)
        for h in range(heads):
            scores = dot(keys, head_rows(own, other, h, head), NT)
            products = dot(values, head_rows(own, other, heads + h, head), NT)
            if masked:
                scores = scores + mask[...]
            rows = scores.shape[1]
            scores = scores.reshape(-1, 8, rows)
            products = products.reshape(-1, 8, rows)
            raised = jnp.maximum(most[h], jnp.max(scores, axis=0))
            fade = jnp.exp2((most[h] - raised) * factor)
            weights = jnp.exp2((scores - raised[None]) * factor)
            most[h] = raised
            total[h] = total[h] * fade + jnp.sum(weights, axis=0)
            weighted[h] = weighted[h] * fade + jnp.sum(weights * products, axis=0)

    visit(0, True)

    @pl.loop(1, info[0] + 1)
    def _(index):
        visit(index, False)

    for h in range(heads):
        top = jnp.max(most[h], axis=0, keepdims=True)
        fade = jnp.exp2((most[h] - top) * factor)
        out[0, h : h + 1] = top
        out[1, h : h + 1] = jnp.sum(total[h] * fade, axis=0, keepdims=True)
        out[2, h : h + 1] = jnp.sum(weighted[h] * fade, axis=0, keepdims=True)


def grads_kernel(
    heads, head, scale, info, own, other, memory, mine, theirs,
    own_grad, other_grad, memory_grad,
    mask, queries, grads, weights_half, slopes_half, query_grad, shift, delta,
):
    groups, block = memory.shape[0] // 2, 2 * memory.shape[2]
    half, rows = block // 2, 2 * block
    factor = scale * LOG2E
    fill_mask(info, mask, block, groups)

    def turned(stat):
        return jnp.concatenate([theirs[stat, :, block:], theirs[stat, :, :block]], axis=1)

    most = [mine[0], turned(0)]
    top = jnp.maximum(most[0], most[1])
    fades = [jnp.exp2((m - top) * factor) for m in most]
    total = mine[1] * fades[0] + turned(1) * fades[1]
    weighted = mine[2] * fades[0] + turned(2) * fades[1]
    shift[...] = top * factor + jnp.log(total) * LOG2E
    delta[...] = weighted / total
    for h in range(heads):
        queries[h * rows : (h + 1) * rows] = head_rows(own, other, h, head)
        grads[h * rows : (h + 1) * rows] = head_rows(own, other, heads + h, head)
    query_grad[...] = jnp.zeros(query_grad.shape, jnp.float32)

    def visit(index, masked):
        keys = group_of(memory, index, head, 0)
        values = group_of(memory, index, head, 1)
        for h in range(heads):
            cut = slice(h * rows, (h + 1) * rows)
            scores = dot(keys, queries[cut], NT)
            products = dot(values, grads[cut], NT)
            if masked:
                scores = scores + mask[...]
            weights = jnp.exp2(scores * factor - shift[h : h + 1])
            slopes = weights * (products - delta[h : h + 1])
            weights_half[:, cut] = weights.astype(jnp.bfloat16)
            slopes_half[:, cut] = slopes.astype(jnp.bfloat16)
        value_grad = dot(weights_half[...], grads[...], NN).astype(jnp.bfloat16)
        key_grad = (dot(slopes_half[...], queries[...], NN) * scale).astype(jnp.bfloat16)
        for g in range(2 * groups):
            cut = slice(g * half, (g + 1) * half)
            memory_grad[g, index, :, :head] = key_grad[cut]
            memory_grad[g, index, :, head:] = value_grad[cut]
        query_grad[...] += dot(keys, slopes_half[...], TN)

    visit(0, True)

    @pl.loop(1, info[0] + 1)
    def _(index):
        visit(index, False)

    for h in range(heads):
        piece = query_grad[:, h * rows : (h + 1) * rows].T * scale
        own_grad[:, h * head : (h + 1) * head] = piece[:block]
        other_grad[:, h * head : (h + 1) * head] = piece[block:].astype(jnp.bfloat16)


def track_kernel(heads, head, scale, span, queries, grads, memory, query_grad, memory_grad):
    tracks, positions, _ = memory.shape
    factor = scale * LOG2E
    key_place = lax.rem(lax.broadcasted_iota(jnp.int32, (tracks * span, heads * span), 0), span)
    row_place = lax.rem(lax.broadcasted_iota(jnp.int32, (tracks * span, heads * span), 1), span)
    mask = jnp.where(key_place == row_place, 0.0, FAR_BELOW)
    for begin in range(0, positions, span):
        at = slice(begin, begin + span)
        rows = jnp.concatenate([queries[at, h * head : (h + 1) * head] for h in range(heads)], axis=0)
        out_rows = jnp.concatenate([grads[at, h * head : (h + 1) * head] for h in range(heads)], axis=0)
        keys = jnp.concatenate([memory[t, at, :head] for t in range(tracks)], axis=0)
        values = jnp.concatenate([memory[t, at, head:] for t in range(tracks)], axis=0)
        scores = dot(keys, rows, NT) + mask
        products = dot(values, out_rows, NT)
        top = jnp.max(scores, axis=0, keepdims=True)
        raw = jnp.exp2((scores - top) * factor)
        inverse = 1.0 / jnp.sum(raw, axis=0, keepdims=True)
        weights = raw * inverse
        delta = jnp.sum(weights * products, axis=0, keepdims=True)
        slopes = weights * (products - delta)
        weights_half = weights.astype(jnp.bfloat16)
        slopes_half = slopes.astype(jnp.bfloat16)
        value_grad = dot(weights_half, out_rows, NN).astype(jnp.bfloat16)
        key_grad = (dot(slopes_half, rows, NN) * scale).astype(jnp.bfloat16)
        row_grad = (dot(keys, slopes_half, TN).T * scale).astype(jnp.bfloat16)
        for t in range(tracks):
            cut = slice(t * span, (t + 1) * span)
            memory_grad[t, at, :head] = key_grad[cut]
            memory_grad[t, at, head:] = value_grad[cut]
        for h in range(heads):
            query_grad[at, h * head : (h + 1) * head] = row_grad[h * span : (h + 1) * span]


def body(time_query, time_memory, time_grad_out, track_query, track_memory, track_grad_out):
    songs, pos_dev, _, feature = time_query.shape
    head = time_memory.shape[3] // 2
    heads = feature // head
    scale = head ** (-0.5)
    block = 2 * pos_dev
    rows = 2 * block
    core = lax.axis_index("core")
    side = lax.axis_index("side")
    low = lax.axis_index("low")
    high = lax.axis_index("high")
    n_low = lax.axis_size("low")
    n_high = lax.axis_size("high")
    tracks = lax.axis_size("track")
    info = jnp.stack([high, low, side, core]).astype(jnp.int32)

    def of_song(array, index):
        return lax.dynamic_index_in_dim(array, index, 0, keepdims=False)

    def places(step):
        pairs = []
        for i in range(n_high - step):
            for j in range(n_low):
                to = n_low - 1 - j if 2 * step == n_high else j
                pairs.append((i * n_low + j, (i + step) * n_low + to))
        return pairs

    memory = time_memory[:, :, 0]
    with jax.named_scope("memory_high"):
        held = [memory]
        for s in range(1, n_high):
            held.append(lax.ppermute(memory, ("high", "low"), places(s)))
    near = held[1]
    held = jnp.stack(held, axis=1)
    with jax.named_scope("query_songs"):
        packed = jnp.concatenate([time_query[:, :, 0], time_grad_out[:, :, 0]], axis=2)
        packed = after(packed, near)
        own = jnp.concatenate(
            [of_song(packed, core), swapped(of_song(packed, 1 - core), "core")], axis=0
        )
    with jax.named_scope("query_sides"):
        other = swapped(own, "side")
    with jax.named_scope("memory_low"):
        held = lax.all_to_all(
            jnp.broadcast_to(held[None], (n_low, *held.shape)).reshape(-1, *held.shape[1:]),
            ("low", "core"), 0, 0, tiled=True,
        )
    bits = [1 << i for i in reversed(range((tracks - 1).bit_length()))]

    def across(array, bit):
        return lax.ppermute(array, "track", [(i, i ^ bit) for i in range(tracks)])

    with jax.named_scope("track_gather"):
        everything = after(track_memory.reshape(1, block, 2 * head), near)
        for bit in bits:
            everything = jnp.concatenate([everything, across(everything, bit)], axis=0)

    mine = pl.pallas_call(
        functools.partial(stats_kernel, heads, head, scale * LOG2E),
        out_shape=jax.ShapeDtypeStruct((3, heads, rows), jnp.float32),
        in_specs=[SMEM] + [VMEM] * 3,
        out_specs=VMEM,
        scratch_shapes=[pltpu.VMEM((n_low * block, rows), jnp.float32)]
        + [pltpu.VMEM((heads, 8, rows), jnp.float32)] * 3,
        compiler_params=PARAMS,
        name="time_stats",
    )(info, own, other, held)
    with jax.named_scope("stats_sides"):
        theirs = swapped(mine, "side")
    track_query_grad, track_partial = pl.pallas_call(
        functools.partial(track_kernel, heads, head, scale, 32),
        out_shape=(
            jax.ShapeDtypeStruct((block, feature), jnp.bfloat16),
            jax.ShapeDtypeStruct((tracks, block, 2 * head), jnp.bfloat16),
        ),
        in_specs=[VMEM] * 3,
        out_specs=(VMEM, VMEM),
        compiler_params=PARAMS,
        name="track_core",
    )(track_query.reshape(block, feature), track_grad_out.reshape(block, feature), after(everything, mine))
    theirs = after(theirs, track_partial)
    own_grad, other_grad, memory_grad = pl.pallas_call(
        functools.partial(grads_kernel, heads, head, scale),
        out_shape=(
            jax.ShapeDtypeStruct((block, feature), jnp.float32),
            jax.ShapeDtypeStruct((block, feature), jnp.bfloat16),
            jax.ShapeDtypeStruct((2 * n_low, n_high, pos_dev, 2 * head), jnp.bfloat16),
        ),
        in_specs=[SMEM] + [VMEM] * 5,
        out_specs=(VMEM, VMEM, VMEM),
        scratch_shapes=[
            pltpu.VMEM((n_low * block, rows), jnp.float32),
            pltpu.VMEM((heads * rows, head), jnp.bfloat16),
            pltpu.VMEM((heads * rows, head), jnp.bfloat16),
            pltpu.VMEM((n_low * block, heads * rows), jnp.bfloat16),
            pltpu.VMEM((n_low * block, heads * rows), jnp.bfloat16),
            pltpu.VMEM((head, heads * rows), jnp.float32),
            pltpu.VMEM((heads, rows), jnp.float32),
            pltpu.VMEM((heads, rows), jnp.float32),
        ],
        compiler_params=PARAMS,
        name="time_grads",
    )(info, own, other, held, mine, theirs)

    with jax.named_scope("memory_grad_low"):
        parts = lax.all_to_all(memory_grad, ("low", "core"), 0, 0, tiled=True)
        parts = parts.reshape(n_low, 2, n_high, pos_dev, 2 * head)
        sums = jnp.sum(parts.astype(jnp.float32), axis=0)
    with jax.named_scope("memory_grad_high"):
        gathered = sums[:, 0]
        for s in range(1, n_high):
            back = lax.ppermute(
                sums[:, s].astype(jnp.bfloat16),
                ("high", "low"),
                [(to, origin) for origin, to in places(s)],
            )
            gathered = gathered + back.astype(jnp.float32)
        time_memory_grad = gathered.astype(jnp.bfloat16).reshape(time_memory.shape)

    def to_songs(array):
        ours = array[:pos_dev]
        back = swapped(array[pos_dev:], "core")
        first = jnp.where(core == 0, ours, back)
        second = jnp.where(core == 0, back, ours)
        return jnp.stack([first, second])[:, :, None, :]

    with jax.named_scope("query_grad_sides"):
        query_grad = own_grad + swapped(other_grad, "side").astype(jnp.float32)
    with jax.named_scope("query_grad_songs"):
        time_query_grad = to_songs(query_grad.astype(jnp.bfloat16))
    with jax.named_scope("track_scatter"):
        partial = track_partial
        for bit in reversed(bits):
            kept, sent = jnp.split(partial, 2)
            back = across(sent.astype(jnp.bfloat16), bit)
            partial = kept.astype(jnp.float32) + back.astype(jnp.float32)
        track_memory_grad = partial.astype(jnp.bfloat16)
    return (
        time_query_grad,
        time_memory_grad,
        track_query_grad.reshape(track_query.shape),
        track_memory_grad.reshape(track_memory.shape),
    )


def solution(mesh):
    tracks, times = mesh.devices.shape
    chips = times // 4
    high = next(n for n in (4, 2, 1) if chips % n == 0)
    axes = ("track", "high", "low", "side", "core")
    finer = Mesh(mesh.devices.reshape(tracks, high, chips // high, 2, 2), axes)
    placed = P(None, axes[1:], "track", None)
    return jax.shard_map(
        body,
        mesh=finer,
        in_specs=(placed,) * 6,
        out_specs=(placed,) * 4,
        check_vma=False,
    )
```

```python
import functools
import math

import jax
import jax.numpy as jnp
from jax import lax
from jax.experimental import pallas as pl
from jax.experimental.pallas import tpu as pltpu
from jax.sharding import Mesh, PartitionSpec as P

FAR_BELOW = -1e30
LOG2E = math.log2(math.e)
NT = (((1,), (1,)), ((), ()))
NN = (((1,), (0,)), ((), ()))
TN = (((0,), (0,)), ((), ()))
VMEM = pl.BlockSpec(memory_space=pltpu.VMEM)
SMEM = pl.BlockSpec(memory_space=pltpu.SMEM)
PARAMS = pltpu.CompilerParams(vmem_limit_bytes=48 * 1024 * 1024)


def dot(a, b, dims):
    return lax.dot_general(a, b, dims, preferred_element_type=jnp.float32)


def after(block, earlier):
    return lax.optimization_barrier((block, earlier))[0]


def swapped(block, axis):
    return lax.ppermute(block, axis, [(0, 1), (1, 0)])


def fill_mask(info, mask, block, groups):
    low, side, core = info[1], info[2], info[3]
    half = block // 2

    def place(index):
        return lax.rem(index + core * half, block)

    key = lax.broadcasted_iota(jnp.int32, (block, block), 0)
    row = lax.broadcasted_iota(jnp.int32, (block, block), 1)
    causal = jnp.where(key <= place(row), 0.0, FAR_BELOW)
    for g in range(groups):
        before = jnp.where(g < low, 0.0, FAR_BELOW)
        at = g == low
        own = jnp.where(at, causal, before)
        other = jnp.where(jnp.logical_and(at, side == 0), 0.0, before)
        mask[g * block : (g + 1) * block, :block] = own
        mask[g * block : (g + 1) * block, block:] = jnp.broadcast_to(other, (block, block))


def group_of(memory, index, head, part):
    pieces = [memory[g, index, :, part * head : (part + 1) * head] for g in range(memory.shape[0])]
    return jnp.concatenate(pieces, axis=0)


def head_rows(own, other, column, head):
    cut = slice(column * head, (column + 1) * head)
    return jnp.concatenate([own[:, cut], other[:, cut]], axis=0)


def stats_kernel(heads, head, factor, info, own, other, memory, out, mask, turned, most, total, weighted):
    groups, block = memory.shape[0] // 2, 2 * memory.shape[2]
    fill_mask(info, mask, block, groups)
    for h in range(2 * heads):
        turned[h] = head_rows(own, other, h, head).T
    most[...] = jnp.full(most.shape, FAR_BELOW, jnp.float32)
    total[...] = jnp.zeros(total.shape, jnp.float32)
    weighted[...] = jnp.zeros(weighted.shape, jnp.float32)

    def visit(index, masked):
        keys = group_of(memory, index, head, 0)
        values = group_of(memory, index, head, 1)
        for h in range(heads):
            most_h, total_h, weighted_h = most[h], total[h], weighted[h]
            for begin in range(0, keys.shape[0], block):
                scores = dot(keys[begin : begin + block], turned[h], NN)
                products = dot(values[begin : begin + block], turned[heads + h], NN)
                if masked:
                    scores = scores + mask[begin : begin + block]
                rows = scores.shape[1]
                scores = scores.reshape(-1, 8, rows)
                products = products.reshape(-1, 8, rows)
                raised = jnp.maximum(most_h, jnp.max(scores, axis=0))
                fade = jnp.exp2((most_h - raised) * factor)
                weights = jnp.exp2((scores - raised[None]) * factor)
                most_h = raised
                total_h = total_h * fade + jnp.sum(weights, axis=0)
                weighted_h = weighted_h * fade + jnp.sum(weights * products, axis=0)
            most[h], total[h], weighted[h] = most_h, total_h, weighted_h

    visit(0, True)

    @pl.loop(memory.shape[1] - info[0], memory.shape[1])
    def _(index):
        visit(index, False)

    for h in range(heads):
        top = jnp.max(most[h], axis=0, keepdims=True)
        fade = jnp.exp2((most[h] - top) * factor)
        out[0, h : h + 1] = top
        out[1, h : h + 1] = jnp.sum(total[h] * fade, axis=0, keepdims=True)
        out[2, h : h + 1] = jnp.sum(weighted[h] * fade, axis=0, keepdims=True)


def grads_kernel(
    heads, head, scale, info, own, other, memory, mine, theirs,
    own_grad, other_grad, memory_grad,
    mask, queries, grads, weights_half, slopes_half, query_grad, shift, delta,
):
    groups, block = memory.shape[0] // 2, 2 * memory.shape[2]
    half, rows = block // 2, 2 * block
    factor = scale * LOG2E
    fill_mask(info, mask, block, groups)

    def turned(stat):
        return jnp.concatenate([theirs[stat, :, block:], theirs[stat, :, :block]], axis=1)

    most = [mine[0], turned(0)]
    top = jnp.maximum(most[0], most[1])
    fades = [jnp.exp2((m - top) * factor) for m in most]
    total = mine[1] * fades[0] + turned(1) * fades[1]
    weighted = mine[2] * fades[0] + turned(2) * fades[1]
    shift[...] = top * factor + jnp.log(total) * LOG2E
    delta[...] = weighted / total
    for h in range(heads):
        queries[h * rows : (h + 1) * rows] = head_rows(own, other, h, head)
        grads[h * rows : (h + 1) * rows] = head_rows(own, other, heads + h, head)
    query_grad[...] = jnp.zeros(query_grad.shape, jnp.float32)

    def visit(index, masked):
        keys = group_of(memory, index, head, 0)
        values = group_of(memory, index, head, 1)
        for h in range(heads):
            cut = slice(h * rows, (h + 1) * rows)
            scores = dot(keys, queries[cut], NT)
            products = dot(values, grads[cut], NT)
            if masked:
                scores = scores + mask[...]
            weights = jnp.exp2(scores * factor - shift[h : h + 1])
            slopes = weights * (products - delta[h : h + 1])
            weights_half[:, cut] = weights.astype(jnp.bfloat16)
            slopes_half[:, cut] = slopes.astype(jnp.bfloat16)
        value_grad = dot(weights_half[...], grads[...], NN).astype(jnp.bfloat16)
        key_grad = (dot(slopes_half[...], queries[...], NN) * scale).astype(jnp.bfloat16)
        for g in range(2 * groups):
            cut = slice(g * half, (g + 1) * half)
            memory_grad[g, index, :, :head] = key_grad[cut]
            memory_grad[g, index, :, head:] = value_grad[cut]
        query_grad[...] += dot(keys, slopes_half[...], TN)

    visit(0, True)

    @pl.loop(memory.shape[1] - info[0], memory.shape[1])
    def _(index):
        visit(index, False)

    for h in range(heads):
        piece = query_grad[:, h * rows : (h + 1) * rows].T * scale
        own_grad[:, h * head : (h + 1) * head] = piece[:block]
        other_grad[:, h * head : (h + 1) * head] = piece[block:].astype(jnp.bfloat16)


def track_kernel(heads, head, scale, span, queries, grads, memory, query_grad, memory_grad):
    tracks, positions, _ = memory.shape
    factor = scale * LOG2E
    key_place = lax.rem(lax.broadcasted_iota(jnp.int32, (tracks * span, heads * span), 0), span)
    row_place = lax.rem(lax.broadcasted_iota(jnp.int32, (tracks * span, heads * span), 1), span)
    mask = jnp.where(key_place == row_place, 0.0, FAR_BELOW)
    for begin in range(0, positions, span):
        at = slice(begin, begin + span)
        rows = jnp.concatenate([queries[at, h * head : (h + 1) * head] for h in range(heads)], axis=0)
        out_rows = jnp.concatenate([grads[at, h * head : (h + 1) * head] for h in range(heads)], axis=0)
        keys = jnp.concatenate([memory[t, at, :head] for t in range(tracks)], axis=0)
        values = jnp.concatenate([memory[t, at, head:] for t in range(tracks)], axis=0)
        scores = dot(keys, rows, NT) + mask
        products = dot(values, out_rows, NT)
        top = jnp.max(scores, axis=0, keepdims=True)
        raw = jnp.exp2((scores - top) * factor)
        inverse = 1.0 / jnp.sum(raw, axis=0, keepdims=True)
        weights = raw * inverse
        delta = jnp.sum(weights * products, axis=0, keepdims=True)
        slopes = weights * (products - delta)
        weights_half = weights.astype(jnp.bfloat16)
        slopes_half = slopes.astype(jnp.bfloat16)
        value_grad = dot(weights_half, out_rows, NN).astype(jnp.bfloat16)
        key_grad = (dot(slopes_half, rows, NN) * scale).astype(jnp.bfloat16)
        row_grad = (dot(keys, slopes_half, TN).T * scale).astype(jnp.bfloat16)
        for t in range(tracks):
            cut = slice(t * span, (t + 1) * span)
            memory_grad[t, at, :head] = key_grad[cut]
            memory_grad[t, at, head:] = value_grad[cut]
        for h in range(heads):
            query_grad[at, h * head : (h + 1) * head] = row_grad[h * span : (h + 1) * span]


def body(time_query, time_memory, time_grad_out, track_query, track_memory, track_grad_out):
    songs, pos_dev, _, feature = time_query.shape
    head = time_memory.shape[3] // 2
    heads = feature // head
    scale = head ** (-0.5)
    block = 2 * pos_dev
    rows = 2 * block
    core = lax.axis_index("core")
    side = lax.axis_index("side")
    low = lax.axis_index("low")
    high = lax.axis_index("high")
    n_low = lax.axis_size("low")
    n_high = lax.axis_size("high")
    tracks = lax.axis_size("track")
    info = jnp.stack([high, low, side, core]).astype(jnp.int32)

    def of_song(array, index):
        return lax.dynamic_index_in_dim(array, index, 0, keepdims=False)

    def places(step):
        pairs = []
        for i in range(n_high - step):
            for j in range(n_low):
                to = n_low - 1 - j if 2 * step == n_high else j
                pairs.append((i * n_low + j, (i + step) * n_low + to))
        return pairs

    memory = time_memory[:, :, 0]
    with jax.named_scope("memory_high"):
        steps = range(n_high - 1, 0, -1)
        held = [memory] + [lax.ppermute(memory, ("high", "low"), places(s)) for s in steps]
    near = held[-1]
    with jax.named_scope("query_songs"):
        packed = jnp.concatenate([time_query[:, :, 0], time_grad_out[:, :, 0]], axis=2)
        packed = after(packed, near)
        own = jnp.concatenate(
            [of_song(packed, core), swapped(of_song(packed, 1 - core), "core")], axis=0
        )
    with jax.named_scope("query_sides"):
        other = swapped(own, "side")
    with jax.named_scope("memory_low"):
        everyone = jnp.stack([jnp.broadcast_to(h[None], (n_low, *h.shape)) for h in held], axis=2)
        held = lax.all_to_all(
            everyone.reshape(-1, *everyone.shape[2:]), ("low", "core"), 0, 0, tiled=True
        )
    bits = [1 << i for i in reversed(range((tracks - 1).bit_length()))]

    def across(array, bit):
        return lax.ppermute(array, "track", [(i, i ^ bit) for i in range(tracks)])

    with jax.named_scope("track_gather"):
        everything = after(track_memory.reshape(1, block, 2 * head), near)
        for bit in bits:
            everything = jnp.concatenate([everything, across(everything, bit)], axis=0)

    mine = pl.pallas_call(
        functools.partial(stats_kernel, heads, head, scale * LOG2E),
        out_shape=jax.ShapeDtypeStruct((3, heads, rows), jnp.float32),
        in_specs=[SMEM] + [VMEM] * 3,
        out_specs=VMEM,
        scratch_shapes=[
            pltpu.VMEM((n_low * block, rows), jnp.float32),
            pltpu.VMEM((2 * heads, head, rows), jnp.bfloat16),
        ]
        + [pltpu.VMEM((heads, 8, rows), jnp.float32)] * 3,
        compiler_params=PARAMS,
        name="time_stats",
    )(info, own, other, held)
    with jax.named_scope("stats_sides"):
        theirs = swapped(mine, "side")
    track_query_grad, track_partial = pl.pallas_call(
        functools.partial(track_kernel, heads, head, scale, 32),
        out_shape=(
            jax.ShapeDtypeStruct((block, feature), jnp.bfloat16),
            jax.ShapeDtypeStruct((tracks, block, 2 * head), jnp.bfloat16),
        ),
        in_specs=[VMEM] * 3,
        out_specs=(VMEM, VMEM),
        compiler_params=PARAMS,
        name="track_core",
    )(track_query.reshape(block, feature), track_grad_out.reshape(block, feature), after(everything, mine))
    theirs = after(theirs, track_partial)
    own_grad, other_grad, memory_grad = pl.pallas_call(
        functools.partial(grads_kernel, heads, head, scale),
        out_shape=(
            jax.ShapeDtypeStruct((block, feature), jnp.float32),
            jax.ShapeDtypeStruct((block, feature), jnp.bfloat16),
            jax.ShapeDtypeStruct((2 * n_low, n_high, pos_dev, 2 * head), jnp.bfloat16),
        ),
        in_specs=[SMEM] + [VMEM] * 5,
        out_specs=(VMEM, VMEM, VMEM),
        scratch_shapes=[
            pltpu.VMEM((n_low * block, rows), jnp.float32),
            pltpu.VMEM((heads * rows, head), jnp.bfloat16),
            pltpu.VMEM((heads * rows, head), jnp.bfloat16),
            pltpu.VMEM((n_low * block, heads * rows), jnp.bfloat16),
            pltpu.VMEM((n_low * block, heads * rows), jnp.bfloat16),
            pltpu.VMEM((head, heads * rows), jnp.float32),
            pltpu.VMEM((heads, rows), jnp.float32),
            pltpu.VMEM((heads, rows), jnp.float32),
        ],
        compiler_params=PARAMS,
        name="time_grads",
    )(info, own, other, held, mine, theirs)

    with jax.named_scope("memory_grad_low"):
        parts = lax.all_to_all(memory_grad, ("low", "core"), 0, 0, tiled=True)
        parts = parts.reshape(n_low, 2, n_high, pos_dev, 2 * head)
        sums = jnp.sum(parts.astype(jnp.float32), axis=0)
    with jax.named_scope("memory_grad_high"):
        gathered = sums[:, 0]
        for s in steps:
            back = lax.ppermute(
                sums[:, n_high - s].astype(jnp.bfloat16),
                ("high", "low"),
                [(to, origin) for origin, to in places(s)],
            )
            gathered = gathered + back.astype(jnp.float32)
        time_memory_grad = gathered.astype(jnp.bfloat16).reshape(time_memory.shape)

    def to_songs(array):
        ours = array[:pos_dev]
        back = swapped(array[pos_dev:], "core")
        first = jnp.where(core == 0, ours, back)
        second = jnp.where(core == 0, back, ours)
        return jnp.stack([first, second])[:, :, None, :]

    with jax.named_scope("query_grad_sides"):
        query_grad = own_grad + swapped(other_grad, "side").astype(jnp.float32)
    with jax.named_scope("query_grad_songs"):
        time_query_grad = to_songs(query_grad.astype(jnp.bfloat16))
    with jax.named_scope("track_scatter"):
        partial = track_partial
        for bit in reversed(bits):
            kept, sent = jnp.split(partial, 2)
            back = across(sent.astype(jnp.bfloat16), bit)
            partial = kept.astype(jnp.float32) + back.astype(jnp.float32)
        track_memory_grad = partial.astype(jnp.bfloat16)
    return (
        time_query_grad,
        time_memory_grad,
        track_query_grad.reshape(track_query.shape),
        track_memory_grad.reshape(track_memory.shape),
    )


def solution(mesh):
    tracks, times = mesh.devices.shape
    chips = times // 4
    high = next(n for n in (4, 2, 1) if chips % n == 0)
    axes = ("track", "high", "low", "side", "core")
    finer = Mesh(mesh.devices.reshape(tracks, high, chips // high, 2, 2), axes)
    placed = P(None, axes[1:], "track", None)
    return jax.shard_map(
        body,
        mesh=finer,
        in_specs=(placed,) * 6,
        out_specs=(placed,) * 4,
        check_vma=False,
    )
```

```python
import functools
import math

import jax
import jax.numpy as jnp
from jax import lax
from jax.experimental import pallas as pl
from jax.experimental.pallas import tpu as pltpu
from jax.sharding import Mesh, PartitionSpec as P

FAR_BELOW = -1e30
LOG2E = math.log2(math.e)
NT = (((1,), (1,)), ((), ()))
NN = (((1,), (0,)), ((), ()))
TN = (((0,), (0,)), ((), ()))
VMEM = pl.BlockSpec(memory_space=pltpu.VMEM)
SMEM = pl.BlockSpec(memory_space=pltpu.SMEM)
PARAMS = pltpu.CompilerParams(vmem_limit_bytes=48 * 1024 * 1024)


def dot(a, b, dims):
    return lax.dot_general(a, b, dims, preferred_element_type=jnp.float32)


def after(block, earlier):
    return lax.optimization_barrier((block, earlier))[0]


def swapped(block, axis):
    return lax.ppermute(block, axis, [(0, 1), (1, 0)])


def half_on(group, place, places):
    return places - 1 - place


def half_back(group, place, places):
    return half_on(group, place, places) if group == 0 else (place - 1) % places


def fill_mask(info, mask, block, groups):
    low, side, core = info[1], info[2], info[3]
    half = block // 2

    def place(index):
        return lax.rem(index + core * half, block)

    key = lax.broadcasted_iota(jnp.int32, (block, block), 0)
    row = lax.broadcasted_iota(jnp.int32, (block, block), 1)
    causal = jnp.where(key <= place(row), 0.0, FAR_BELOW)
    for g in range(groups):
        before = jnp.where(g < low, 0.0, FAR_BELOW)
        at = g == low
        own = jnp.where(at, causal, before)
        other = jnp.where(jnp.logical_and(at, side == 0), 0.0, before)
        mask[g * block : (g + 1) * block, :block] = own
        mask[g * block : (g + 1) * block, block:] = jnp.broadcast_to(other, (block, block))


def group_of(memory, index, head, part):
    pieces = [memory[g, index, :, part * head : (part + 1) * head] for g in range(memory.shape[0])]
    return jnp.concatenate(pieces, axis=0)


def head_rows(own, other, column, head):
    cut = slice(column * head, (column + 1) * head)
    return jnp.concatenate([own[:, cut], other[:, cut]], axis=0)


def stats_kernel(heads, head, factor, info, own, other, memory, out, mask, turned, most, total, weighted):
    groups, block = memory.shape[0] // 2, 2 * memory.shape[2]
    fill_mask(info, mask, block, groups)
    for h in range(2 * heads):
        turned[h] = head_rows(own, other, h, head).T
    most[...] = jnp.full(most.shape, FAR_BELOW, jnp.float32)
    total[...] = jnp.zeros(total.shape, jnp.float32)
    weighted[...] = jnp.zeros(weighted.shape, jnp.float32)

    def visit(index, masked):
        keys = group_of(memory, index, head, 0)
        values = group_of(memory, index, head, 1)
        for h in range(heads):
            most_h, total_h, weighted_h = most[h], total[h], weighted[h]
            for begin in range(0, keys.shape[0], block):
                scores = dot(keys[begin : begin + block], turned[h], NN)
                products = dot(values[begin : begin + block], turned[heads + h], NN)
                if masked:
                    scores = scores + mask[begin : begin + block]
                rows = scores.shape[1]
                scores = scores.reshape(-1, 8, rows)
                products = products.reshape(-1, 8, rows)
                raised = jnp.maximum(most_h, jnp.max(scores, axis=0))
                fade = jnp.exp2((most_h - raised) * factor)
                weights = jnp.exp2((scores - raised[None]) * factor)
                most_h = raised
                total_h = total_h * fade + jnp.sum(weights, axis=0)
                weighted_h = weighted_h * fade + jnp.sum(weights * products, axis=0)
            most[h], total[h], weighted[h] = most_h, total_h, weighted_h

    visit(0, True)

    @pl.loop(memory.shape[1] - info[0], memory.shape[1])
    def _(index):
        visit(index, False)

    for h in range(heads):
        top = jnp.max(most[h], axis=0, keepdims=True)
        fade = jnp.exp2((most[h] - top) * factor)
        out[0, h : h + 1] = top
        out[1, h : h + 1] = jnp.sum(total[h] * fade, axis=0, keepdims=True)
        out[2, h : h + 1] = jnp.sum(weighted[h] * fade, axis=0, keepdims=True)


def grads_kernel(
    heads, head, scale, info, own, other, memory, mine, theirs,
    own_grad, other_grad, memory_grad,
    mask, queries, grads, weights_half, slopes_half, query_grad, shift, delta,
):
    groups, block = memory.shape[0] // 2, 2 * memory.shape[2]
    half, rows = block // 2, 2 * block
    factor = scale * LOG2E
    fill_mask(info, mask, block, groups)

    def turned(stat):
        return jnp.concatenate([theirs[stat, :, block:], theirs[stat, :, :block]], axis=1)

    most = [mine[0], turned(0)]
    top = jnp.maximum(most[0], most[1])
    fades = [jnp.exp2((m - top) * factor) for m in most]
    total = mine[1] * fades[0] + turned(1) * fades[1]
    weighted = mine[2] * fades[0] + turned(2) * fades[1]
    shift[...] = top * factor + jnp.log(total) * LOG2E
    delta[...] = weighted / total
    for h in range(heads):
        queries[h * rows : (h + 1) * rows] = head_rows(own, other, h, head)
        grads[h * rows : (h + 1) * rows] = head_rows(own, other, heads + h, head)
    query_grad[...] = jnp.zeros(query_grad.shape, jnp.float32)

    def visit(index, masked):
        keys = group_of(memory, index, head, 0)
        values = group_of(memory, index, head, 1)
        for h in range(heads):
            cut = slice(h * rows, (h + 1) * rows)
            scores = dot(keys, queries[cut], NT)
            products = dot(values, grads[cut], NT)
            if masked:
                scores = scores + mask[...]
            weights = jnp.exp2(scores * factor - shift[h : h + 1])
            slopes = weights * (products - delta[h : h + 1])
            weights_half[:, cut] = weights.astype(jnp.bfloat16)
            slopes_half[:, cut] = slopes.astype(jnp.bfloat16)
        value_grad = dot(weights_half[...], grads[...], NN).astype(jnp.bfloat16)
        key_grad = (dot(slopes_half[...], queries[...], NN) * scale).astype(jnp.bfloat16)
        for g in range(2 * groups):
            cut = slice(g * half, (g + 1) * half)
            moved = jnp.logical_and(2 * index == memory.shape[1], info[0] == memory.shape[1] - 1)
            leaves = 2 * half_back(1, half_on(1, g // 2, groups), groups) + g % 2
            to = jnp.where(moved, leaves, g)
            memory_grad[to, index, :, :head] = key_grad[cut]
            memory_grad[to, index, :, head:] = value_grad[cut]
        query_grad[...] += dot(keys, slopes_half[...], TN)

    visit(0, True)

    @pl.loop(memory.shape[1] - info[0], memory.shape[1])
    def _(index):
        visit(index, False)

    for h in range(heads):
        piece = query_grad[:, h * rows : (h + 1) * rows].T * scale
        own_grad[:, h * head : (h + 1) * head] = piece[:block]
        other_grad[:, h * head : (h + 1) * head] = piece[block:].astype(jnp.bfloat16)


def track_kernel(heads, head, scale, span, queries, grads, memory, query_grad, memory_grad):
    tracks, positions, _ = memory.shape
    factor = scale * LOG2E
    key_place = lax.rem(lax.broadcasted_iota(jnp.int32, (tracks * span, heads * span), 0), span)
    row_place = lax.rem(lax.broadcasted_iota(jnp.int32, (tracks * span, heads * span), 1), span)
    mask = jnp.where(key_place == row_place, 0.0, FAR_BELOW)
    for begin in range(0, positions, span):
        at = slice(begin, begin + span)
        rows = jnp.concatenate([queries[at, h * head : (h + 1) * head] for h in range(heads)], axis=0)
        out_rows = jnp.concatenate([grads[at, h * head : (h + 1) * head] for h in range(heads)], axis=0)
        keys = jnp.concatenate([memory[t, at, :head] for t in range(tracks)], axis=0)
        values = jnp.concatenate([memory[t, at, head:] for t in range(tracks)], axis=0)
        scores = dot(keys, rows, NT) + mask
        products = dot(values, out_rows, NT)
        top = jnp.max(scores, axis=0, keepdims=True)
        raw = jnp.exp2((scores - top) * factor)
        inverse = 1.0 / jnp.sum(raw, axis=0, keepdims=True)
        weights = raw * inverse
        delta = jnp.sum(weights * products, axis=0, keepdims=True)
        slopes = weights * (products - delta)
        weights_half = weights.astype(jnp.bfloat16)
        slopes_half = slopes.astype(jnp.bfloat16)
        value_grad = dot(weights_half, out_rows, NN).astype(jnp.bfloat16)
        key_grad = (dot(slopes_half, rows, NN) * scale).astype(jnp.bfloat16)
        row_grad = (dot(keys, slopes_half, TN).T * scale).astype(jnp.bfloat16)
        for t in range(tracks):
            cut = slice(t * span, (t + 1) * span)
            memory_grad[t, at, :head] = key_grad[cut]
            memory_grad[t, at, head:] = value_grad[cut]
        for h in range(heads):
            query_grad[at, h * head : (h + 1) * head] = row_grad[h * span : (h + 1) * span]


def body(time_query, time_memory, time_grad_out, track_query, track_memory, track_grad_out):
    songs, pos_dev, _, feature = time_query.shape
    head = time_memory.shape[3] // 2
    heads = feature // head
    scale = head ** (-0.5)
    block = 2 * pos_dev
    rows = 2 * block
    core = lax.axis_index("core")
    side = lax.axis_index("side")
    low = lax.axis_index("low")
    high = lax.axis_index("high")
    n_low = lax.axis_size("low")
    n_high = lax.axis_size("high")
    tracks = lax.axis_size("track")
    info = jnp.stack([high, low, side, core]).astype(jnp.int32)

    def of_song(array, index):
        return lax.dynamic_index_in_dim(array, index, 0, keepdims=False)

    def places(step, half_ring):
        pairs = []
        for i in range(n_high - step):
            for j in range(n_low):
                to = half_ring(i, j, n_low) if 2 * step == n_high else j
                pairs.append((i * n_low + j, (i + step) * n_low + to))
        return pairs

    memory = time_memory[:, :, 0]
    with jax.named_scope("memory_high"):
        steps = range(n_high - 1, 0, -1)
        held = [memory] + [lax.ppermute(memory, ("high", "low"), places(s, half_on)) for s in steps]
    near = held[-1]
    with jax.named_scope("query_songs"):
        packed = jnp.concatenate([time_query[:, :, 0], time_grad_out[:, :, 0]], axis=2)
        packed = after(packed, near)
        own = jnp.concatenate(
            [of_song(packed, core), swapped(of_song(packed, 1 - core), "core")], axis=0
        )
    with jax.named_scope("query_sides"):
        other = swapped(own, "side")
    with jax.named_scope("memory_low"):
        everyone = jnp.stack([jnp.broadcast_to(h[None], (n_low, *h.shape)) for h in held], axis=2)
        held = lax.all_to_all(
            everyone.reshape(-1, *everyone.shape[2:]), ("low", "core"), 0, 0, tiled=True
        )
    bits = [1 << i for i in reversed(range((tracks - 1).bit_length()))]

    def across(array, bit):
        return lax.ppermute(array, "track", [(i, i ^ bit) for i in range(tracks)])

    with jax.named_scope("track_gather"):
        everything = after(track_memory.reshape(1, block, 2 * head), near)
        for bit in bits:
            everything = jnp.concatenate([everything, across(everything, bit)], axis=0)

    mine = pl.pallas_call(
        functools.partial(stats_kernel, heads, head, scale * LOG2E),
        out_shape=jax.ShapeDtypeStruct((3, heads, rows), jnp.float32),
        in_specs=[SMEM] + [VMEM] * 3,
        out_specs=VMEM,
        scratch_shapes=[
            pltpu.VMEM((n_low * block, rows), jnp.float32),
            pltpu.VMEM((2 * heads, head, rows), jnp.bfloat16),
        ]
        + [pltpu.VMEM((heads, 8, rows), jnp.float32)] * 3,
        compiler_params=PARAMS,
        name="time_stats",
    )(info, own, other, held)
    with jax.named_scope("stats_sides"):
        theirs = swapped(mine, "side")
    track_query_grad, track_partial = pl.pallas_call(
        functools.partial(track_kernel, heads, head, scale, 32),
        out_shape=(
            jax.ShapeDtypeStruct((block, feature), jnp.bfloat16),
            jax.ShapeDtypeStruct((tracks, block, 2 * head), jnp.bfloat16),
        ),
        in_specs=[VMEM] * 3,
        out_specs=(VMEM, VMEM),
        compiler_params=PARAMS,
        name="track_core",
    )(track_query.reshape(block, feature), track_grad_out.reshape(block, feature), after(everything, mine))
    theirs = after(theirs, track_partial)
    own_grad, other_grad, memory_grad = pl.pallas_call(
        functools.partial(grads_kernel, heads, head, scale),
        out_shape=(
            jax.ShapeDtypeStruct((block, feature), jnp.float32),
            jax.ShapeDtypeStruct((block, feature), jnp.bfloat16),
            jax.ShapeDtypeStruct((2 * n_low, n_high, pos_dev, 2 * head), jnp.bfloat16),
        ),
        in_specs=[SMEM] + [VMEM] * 5,
        out_specs=(VMEM, VMEM, VMEM),
        scratch_shapes=[
            pltpu.VMEM((n_low * block, rows), jnp.float32),
            pltpu.VMEM((heads * rows, head), jnp.bfloat16),
            pltpu.VMEM((heads * rows, head), jnp.bfloat16),
            pltpu.VMEM((n_low * block, heads * rows), jnp.bfloat16),
            pltpu.VMEM((n_low * block, heads * rows), jnp.bfloat16),
            pltpu.VMEM((head, heads * rows), jnp.float32),
            pltpu.VMEM((heads, rows), jnp.float32),
            pltpu.VMEM((heads, rows), jnp.float32),
        ],
        compiler_params=PARAMS,
        name="time_grads",
    )(info, own, other, held, mine, theirs)

    with jax.named_scope("memory_grad_low"):
        parts = lax.all_to_all(memory_grad, ("low", "core"), 0, 0, tiled=True)
        parts = parts.reshape(n_low, 2, n_high, pos_dev, 2 * head)
        sums = jnp.sum(parts.astype(jnp.float32), axis=0)
    with jax.named_scope("memory_grad_high"):
        gathered = sums[:, 0]
        for s in (3, 2, 1):
            came = lax.ppermute(
                sums[:, n_high - s].astype(jnp.bfloat16),
                ("high", "low"),
                [(to, origin) for origin, to in places(s, half_back)],
            )
            gathered = gathered + came.astype(jnp.float32)
        time_memory_grad = gathered.astype(jnp.bfloat16).reshape(time_memory.shape)

    def to_songs(array):
        ours = array[:pos_dev]
        back = swapped(array[pos_dev:], "core")
        first = jnp.where(core == 0, ours, back)
        second = jnp.where(core == 0, back, ours)
        return jnp.stack([first, second])[:, :, None, :]

    with jax.named_scope("query_grad_sides"):
        query_grad = own_grad + swapped(other_grad, "side").astype(jnp.float32)
    with jax.named_scope("query_grad_songs"):
        time_query_grad = to_songs(query_grad.astype(jnp.bfloat16))
    with jax.named_scope("track_scatter"):
        partial = track_partial
        for bit in reversed(bits):
            kept, sent = jnp.split(partial, 2)
            back = across(sent.astype(jnp.bfloat16), bit)
            partial = kept.astype(jnp.float32) + back.astype(jnp.float32)
        track_memory_grad = partial.astype(jnp.bfloat16)
    return (
        time_query_grad,
        time_memory_grad,
        track_query_grad.reshape(track_query.shape),
        track_memory_grad.reshape(track_memory.shape),
    )


def solution(mesh):
    tracks, times = mesh.devices.shape
    chips = times // 4
    high = next(n for n in (4, 2, 1) if chips % n == 0)
    axes = ("track", "high", "low", "side", "core")
    finer = Mesh(mesh.devices.reshape(tracks, high, chips // high, 2, 2), axes)
    placed = P(None, axes[1:], "track", None)
    return jax.shard_map(
        body,
        mesh=finer,
        in_specs=(placed,) * 6,
        out_specs=(placed,) * 4,
        check_vma=False,
    )
```

```python
import functools
import math

import jax
import jax.numpy as jnp
from jax import lax
from jax.experimental import pallas as pl
from jax.experimental.pallas import tpu as pltpu
from jax.sharding import Mesh, PartitionSpec as P

FAR_BELOW = -1e30
LOG2E = math.log2(math.e)
NT = (((1,), (1,)), ((), ()))
NN = (((1,), (0,)), ((), ()))
TN = (((0,), (0,)), ((), ()))
VMEM = pl.BlockSpec(memory_space=pltpu.VMEM)
SMEM = pl.BlockSpec(memory_space=pltpu.SMEM)
PARAMS = pltpu.CompilerParams(vmem_limit_bytes=48 * 1024 * 1024)


def dot(a, b, dims):
    return lax.dot_general(a, b, dims, preferred_element_type=jnp.float32)


def after(block, earlier):
    return lax.optimization_barrier((block, earlier))[0]


def swapped(block, axis):
    return lax.ppermute(block, axis, [(0, 1), (1, 0)])


def half_on(group, place, places):
    return places - 1 - place


def half_back(group, place, places):
    return half_on(group, place, places) if group == 0 else (place - 1) % places


def fill_mask(info, mask, block, groups):
    low, side, core = info[1], info[2], info[3]
    half = block // 2

    def place(index):
        return lax.rem(index + core * half, block)

    key = lax.broadcasted_iota(jnp.int32, (block, block), 0)
    row = lax.broadcasted_iota(jnp.int32, (block, block), 1)
    causal = jnp.where(key <= place(row), 0.0, FAR_BELOW)
    for g in range(groups):
        before = jnp.where(g < low, 0.0, FAR_BELOW)
        at = g == low
        own = jnp.where(at, causal, before)
        other = jnp.where(jnp.logical_and(at, side == 0), 0.0, before)
        mask[g * block : (g + 1) * block, :block] = own
        mask[g * block : (g + 1) * block, block:] = jnp.broadcast_to(other, (block, block))


def group_of(memory, index, head, part):
    pieces = [memory[g, index, :, part * head : (part + 1) * head] for g in range(memory.shape[0])]
    return jnp.concatenate(pieces, axis=0)


def head_rows(own, other, column, head):
    cut = slice(column * head, (column + 1) * head)
    return jnp.concatenate([own[:, cut], other[:, cut]], axis=0)


def stats_kernel(heads, head, factor, info, own, other, memory, out, mask, turned, most, total, weighted):
    groups, block = memory.shape[0] // 2, 2 * memory.shape[2]
    fill_mask(info, mask, block, groups)
    for h in range(2 * heads):
        turned[h] = head_rows(own, other, h, head).T
    most[...] = jnp.full(most.shape, FAR_BELOW, jnp.float32)
    total[...] = jnp.zeros(total.shape, jnp.float32)
    weighted[...] = jnp.zeros(weighted.shape, jnp.float32)

    def visit(index, masked):
        keys = group_of(memory, index, head, 0)
        values = group_of(memory, index, head, 1)
        for h in range(heads):
            most_h, total_h, weighted_h = most[h], total[h], weighted[h]
            for begin in range(0, keys.shape[0], block):
                scores = dot(keys[begin : begin + block], turned[h], NN)
                products = dot(values[begin : begin + block], turned[heads + h], NN)
                if masked:
                    scores = scores + mask[begin : begin + block]
                rows = scores.shape[1]
                scores = scores.reshape(-1, 8, rows)
                products = products.reshape(-1, 8, rows)
                raised = jnp.maximum(most_h, jnp.max(scores, axis=0))
                fade = jnp.exp2((most_h - raised) * factor)
                weights = jnp.exp2((scores - raised[None]) * factor)
                most_h = raised
                total_h = total_h * fade + jnp.sum(weights, axis=0)
                weighted_h = weighted_h * fade + jnp.sum(weights * products, axis=0)
            most[h], total[h], weighted[h] = most_h, total_h, weighted_h

    visit(0, True)

    @pl.loop(memory.shape[1] - info[0], memory.shape[1])
    def _(index):
        visit(index, False)

    for h in range(heads):
        top = jnp.max(most[h], axis=0, keepdims=True)
        fade = jnp.exp2((most[h] - top) * factor)
        out[0, h : h + 1] = top
        out[1, h : h + 1] = jnp.sum(total[h] * fade, axis=0, keepdims=True)
        out[2, h : h + 1] = jnp.sum(weighted[h] * fade, axis=0, keepdims=True)


def grads_kernel(
    heads, head, scale, info, own, other, memory, mine, theirs,
    own_grad, other_grad, memory_grad,
    mask, queries, grads, weights_half, slopes_half, query_grad, shift, delta,
):
    groups, block = memory.shape[0] // 2, 2 * memory.shape[2]
    half, rows = block // 2, 2 * block
    factor = scale * LOG2E
    fill_mask(info, mask, block, groups)

    def turned(stat):
        return jnp.concatenate([theirs[stat, :, block:], theirs[stat, :, :block]], axis=1)

    most = [mine[0], turned(0)]
    top = jnp.maximum(most[0], most[1])
    fades = [jnp.exp2((m - top) * factor) for m in most]
    total = mine[1] * fades[0] + turned(1) * fades[1]
    weighted = mine[2] * fades[0] + turned(2) * fades[1]
    shift[...] = top * factor + jnp.log(total) * LOG2E
    delta[...] = weighted / total
    for h in range(heads):
        queries[h * rows : (h + 1) * rows] = head_rows(own, other, h, head)
        grads[h * rows : (h + 1) * rows] = head_rows(own, other, heads + h, head)
    query_grad[...] = jnp.zeros(query_grad.shape, jnp.float32)

    def visit(index, masked):
        keys = group_of(memory, index, head, 0)
        values = group_of(memory, index, head, 1)
        for h in range(heads):
            cut = slice(h * rows, (h + 1) * rows)
            scores = dot(keys, queries[cut], NT)
            products = dot(values, grads[cut], NT)
            if masked:
                scores = scores + mask[...]
            weights = jnp.exp2(scores * factor - shift[h : h + 1])
            slopes = weights * (products - delta[h : h + 1])
            weights_half[:, cut] = weights.astype(jnp.bfloat16)
            slopes_half[:, cut] = slopes.astype(jnp.bfloat16)
        value_grad = dot(weights_half[...], grads[...], NN).astype(jnp.bfloat16)
        key_grad = (dot(slopes_half[...], queries[...], NN) * scale).astype(jnp.bfloat16)
        for g in range(2 * groups):
            cut = slice(g * half, (g + 1) * half)
            moved = jnp.logical_and(2 * index == memory.shape[1], info[0] == memory.shape[1] - 1)
            leaves = 2 * half_back(1, half_on(1, g // 2, groups), groups) + g % 2
            to = jnp.where(moved, leaves, g)
            memory_grad[to, index, :, :head] = key_grad[cut]
            memory_grad[to, index, :, head:] = value_grad[cut]
        query_grad[...] += dot(keys, slopes_half[...], TN)

    visit(0, True)

    @pl.loop(memory.shape[1] - info[0], memory.shape[1])
    def _(index):
        visit(index, False)

    for h in range(heads):
        piece = query_grad[:, h * rows : (h + 1) * rows].T * scale
        own_grad[:, h * head : (h + 1) * head] = piece[:block]
        other_grad[:, h * head : (h + 1) * head] = piece[block:].astype(jnp.bfloat16)


def track_kernel(heads, head, scale, span, queries, grads, memory, query_grad, memory_grad):
    tracks, positions, _ = memory.shape
    factor = scale * LOG2E
    key_place = lax.rem(lax.broadcasted_iota(jnp.int32, (tracks * span, heads * span), 0), span)
    row_place = lax.rem(lax.broadcasted_iota(jnp.int32, (tracks * span, heads * span), 1), span)
    mask = jnp.where(key_place == row_place, 0.0, FAR_BELOW)
    for begin in range(0, positions, span):
        at = slice(begin, begin + span)
        rows = jnp.concatenate([queries[at, h * head : (h + 1) * head] for h in range(heads)], axis=0)
        out_rows = jnp.concatenate([grads[at, h * head : (h + 1) * head] for h in range(heads)], axis=0)
        keys = jnp.concatenate([memory[t, at, :head] for t in range(tracks)], axis=0)
        values = jnp.concatenate([memory[t, at, head:] for t in range(tracks)], axis=0)
        scores = dot(keys, rows, NT) + mask
        products = dot(values, out_rows, NT)
        top = jnp.max(scores, axis=0, keepdims=True)
        raw = jnp.exp2((scores - top) * factor)
        inverse = 1.0 / jnp.sum(raw, axis=0, keepdims=True)
        weights = raw * inverse
        delta = jnp.sum(weights * products, axis=0, keepdims=True)
        slopes = weights * (products - delta)
        weights_half = weights.astype(jnp.bfloat16)
        slopes_half = slopes.astype(jnp.bfloat16)
        value_grad = dot(weights_half, out_rows, NN).astype(jnp.bfloat16)
        key_grad = (dot(slopes_half, rows, NN) * scale).astype(jnp.bfloat16)
        row_grad = (dot(keys, slopes_half, TN).T * scale).astype(jnp.bfloat16)
        for t in range(tracks):
            cut = slice(t * span, (t + 1) * span)
            memory_grad[t, at, :head] = key_grad[cut]
            memory_grad[t, at, head:] = value_grad[cut]
        for h in range(heads):
            query_grad[at, h * head : (h + 1) * head] = row_grad[h * span : (h + 1) * span]


def body(time_query, time_memory, time_grad_out, track_query, track_memory, track_grad_out):
    songs, pos_dev, _, feature = time_query.shape
    head = time_memory.shape[3] // 2
    heads = feature // head
    scale = head ** (-0.5)
    block = 2 * pos_dev
    rows = 2 * block
    core = lax.axis_index("core")
    side = lax.axis_index("side")
    low = lax.axis_index("low")
    high = lax.axis_index("high")
    n_low = lax.axis_size("low")
    n_high = lax.axis_size("high")
    tracks = lax.axis_size("track")
    info = jnp.stack([high, low, side, core]).astype(jnp.int32)

    def of_song(array, index):
        return lax.dynamic_index_in_dim(array, index, 0, keepdims=False)

    def places(step, half_ring):
        pairs = []
        for i in range(n_high - step):
            for j in range(n_low):
                to = half_ring(i, j, n_low) if 2 * step == n_high else j
                pairs.append((i * n_low + j, (i + step) * n_low + to))
        return pairs

    memory = time_memory[:, :, 0]
    with jax.named_scope("memory_high"):
        steps = range(n_high - 1, 0, -1)
        held = [memory] + [lax.ppermute(memory, ("high", "low"), places(s, half_on)) for s in steps]
    near = held[-1]
    with jax.named_scope("query_songs"):
        packed = jnp.concatenate([time_query[:, :, 0], time_grad_out[:, :, 0]], axis=2)
        packed = after(packed, held[1])
        own = jnp.concatenate(
            [of_song(packed, core), swapped(of_song(packed, 1 - core), "core")], axis=0
        )
    with jax.named_scope("query_sides"):
        other = swapped(own, "side")
    with jax.named_scope("memory_low"):
        everyone = jnp.stack([jnp.broadcast_to(h[None], (n_low, *h.shape)) for h in held], axis=2)
        held = lax.all_to_all(
            everyone.reshape(-1, *everyone.shape[2:]), ("low", "core"), 0, 0, tiled=True
        )
    bits = [1 << i for i in reversed(range((tracks - 1).bit_length()))]

    def across(array, bit):
        return lax.ppermute(array, "track", [(i, i ^ bit) for i in range(tracks)])

    with jax.named_scope("track_gather"):
        everything = after(track_memory.reshape(1, block, 2 * head), near)
        for bit in bits:
            everything = jnp.concatenate([everything, across(everything, bit)], axis=0)

    mine = pl.pallas_call(
        functools.partial(stats_kernel, heads, head, scale * LOG2E),
        out_shape=jax.ShapeDtypeStruct((3, heads, rows), jnp.float32),
        in_specs=[SMEM] + [VMEM] * 3,
        out_specs=VMEM,
        scratch_shapes=[
            pltpu.VMEM((n_low * block, rows), jnp.float32),
            pltpu.VMEM((2 * heads, head, rows), jnp.bfloat16),
        ]
        + [pltpu.VMEM((heads, 8, rows), jnp.float32)] * 3,
        compiler_params=PARAMS,
        name="time_stats",
    )(info, own, other, held)
    with jax.named_scope("stats_sides"):
        theirs = swapped(mine, "side")
    track_query_grad, track_partial = pl.pallas_call(
        functools.partial(track_kernel, heads, head, scale, 32),
        out_shape=(
            jax.ShapeDtypeStruct((block, feature), jnp.bfloat16),
            jax.ShapeDtypeStruct((tracks, block, 2 * head), jnp.bfloat16),
        ),
        in_specs=[VMEM] * 3,
        out_specs=(VMEM, VMEM),
        compiler_params=PARAMS,
        name="track_core",
    )(track_query.reshape(block, feature), track_grad_out.reshape(block, feature), after(everything, mine))
    theirs = after(theirs, track_partial)
    own_grad, other_grad, memory_grad = pl.pallas_call(
        functools.partial(grads_kernel, heads, head, scale),
        out_shape=(
            jax.ShapeDtypeStruct((block, feature), jnp.float32),
            jax.ShapeDtypeStruct((block, feature), jnp.bfloat16),
            jax.ShapeDtypeStruct((2 * n_low, n_high, pos_dev, 2 * head), jnp.bfloat16),
        ),
        in_specs=[SMEM] + [VMEM] * 5,
        out_specs=(VMEM, VMEM, VMEM),
        scratch_shapes=[
            pltpu.VMEM((n_low * block, rows), jnp.float32),
            pltpu.VMEM((heads * rows, head), jnp.bfloat16),
            pltpu.VMEM((heads * rows, head), jnp.bfloat16),
            pltpu.VMEM((n_low * block, heads * rows), jnp.bfloat16),
            pltpu.VMEM((n_low * block, heads * rows), jnp.bfloat16),
            pltpu.VMEM((head, heads * rows), jnp.float32),
            pltpu.VMEM((heads, rows), jnp.float32),
            pltpu.VMEM((heads, rows), jnp.float32),
        ],
        compiler_params=PARAMS,
        name="time_grads",
    )(info, own, other, held, mine, theirs)

    with jax.named_scope("memory_grad_low"):
        parts = lax.all_to_all(memory_grad, ("low", "core"), 0, 0, tiled=True)
        parts = parts.reshape(n_low, 2, n_high, pos_dev, 2 * head)
        sums = jnp.sum(parts.astype(jnp.float32), axis=0)
    with jax.named_scope("memory_grad_high"):
        gathered = sums[:, 0]
        for s in (3, 2, 1):
            came = lax.ppermute(
                sums[:, n_high - s].astype(jnp.bfloat16),
                ("high", "low"),
                [(to, origin) for origin, to in places(s, half_back)],
            )
            gathered = gathered + came.astype(jnp.float32)
        time_memory_grad = gathered.astype(jnp.bfloat16).reshape(time_memory.shape)

    def to_songs(array):
        ours = array[:pos_dev]
        back = swapped(array[pos_dev:], "core")
        first = jnp.where(core == 0, ours, back)
        second = jnp.where(core == 0, back, ours)
        return jnp.stack([first, second])[:, :, None, :]

    with jax.named_scope("query_grad_sides"):
        query_grad = own_grad + swapped(other_grad, "side").astype(jnp.float32)
    with jax.named_scope("query_grad_songs"):
        time_query_grad = to_songs(query_grad.astype(jnp.bfloat16))
    with jax.named_scope("track_scatter"):
        partial = track_partial
        for bit in reversed(bits):
            kept, sent = jnp.split(partial, 2)
            back = across(sent.astype(jnp.bfloat16), bit)
            partial = kept.astype(jnp.float32) + back.astype(jnp.float32)
        track_memory_grad = partial.astype(jnp.bfloat16)
    return (
        time_query_grad,
        time_memory_grad,
        track_query_grad.reshape(track_query.shape),
        track_memory_grad.reshape(track_memory.shape),
    )


def solution(mesh):
    tracks, times = mesh.devices.shape
    chips = times // 4
    high = next(n for n in (4, 2, 1) if chips % n == 0)
    axes = ("track", "high", "low", "side", "core")
    finer = Mesh(mesh.devices.reshape(tracks, high, chips // high, 2, 2), axes)
    placed = P(None, axes[1:], "track", None)
    return jax.shard_map(
        body,
        mesh=finer,
        in_specs=(placed,) * 6,
        out_specs=(placed,) * 4,
        check_vma=False,
    )
```

```python
import functools
import math

import jax
import jax.numpy as jnp
from jax import lax
from jax.experimental import pallas as pl
from jax.experimental.pallas import tpu as pltpu
from jax.sharding import Mesh, PartitionSpec as P

FAR_BELOW = -1e30
LOG2E = math.log2(math.e)
NT = (((1,), (1,)), ((), ()))
NN = (((1,), (0,)), ((), ()))
TN = (((0,), (0,)), ((), ()))
VMEM = pl.BlockSpec(memory_space=pltpu.VMEM)
SMEM = pl.BlockSpec(memory_space=pltpu.SMEM)
PARAMS = pltpu.CompilerParams(vmem_limit_bytes=48 * 1024 * 1024)


def dot(a, b, dims):
    return lax.dot_general(a, b, dims, preferred_element_type=jnp.float32)


def after(block, earlier):
    return lax.optimization_barrier((block, earlier))[0]


def swapped(block, axis):
    return lax.ppermute(block, axis, [(0, 1), (1, 0)])


def half_on(group, place, places):
    return places - 1 - place


def half_back(group, place, places):
    return half_on(group, place, places) if group == 0 else (place - 1) % places


def fill_mask(info, mask, block, groups):
    low, side, core = info[1], info[2], info[3]
    half = block // 2

    def place(index):
        return lax.rem(index + core * half, block)

    key = lax.broadcasted_iota(jnp.int32, (block, block), 0)
    row = lax.broadcasted_iota(jnp.int32, (block, block), 1)
    causal = jnp.where(key <= place(row), 0.0, FAR_BELOW)
    for g in range(groups):
        before = jnp.where(g < low, 0.0, FAR_BELOW)
        at = g == low
        own = jnp.where(at, causal, before)
        other = jnp.where(jnp.logical_and(at, side == 0), 0.0, before)
        mask[g * block : (g + 1) * block, :block] = own
        mask[g * block : (g + 1) * block, block:] = jnp.broadcast_to(other, (block, block))


def group_of(memory, index, head, part):
    pieces = [memory[g, index, :, part * head : (part + 1) * head] for g in range(memory.shape[0])]
    return jnp.concatenate(pieces, axis=0)


def head_rows(own, other, column, head):
    cut = slice(column * head, (column + 1) * head)
    return jnp.concatenate([own[:, cut], other[:, cut]], axis=0)


def stats_kernel(heads, head, factor, info, own, other, memory, out, mask, turned, most, total, weighted):
    groups, block = memory.shape[0] // 2, 2 * memory.shape[2]
    fill_mask(info, mask, block, groups)
    for h in range(2 * heads):
        turned[h] = head_rows(own, other, h, head).T
    most[...] = jnp.full(most.shape, FAR_BELOW, jnp.float32)
    total[...] = jnp.zeros(total.shape, jnp.float32)
    weighted[...] = jnp.zeros(weighted.shape, jnp.float32)

    def visit(index, masked):
        keys = group_of(memory, index, head, 0)
        values = group_of(memory, index, head, 1)
        for h in range(heads):
            most_h, total_h, weighted_h = most[h], total[h], weighted[h]
            for begin in range(0, keys.shape[0], block):
                scores = dot(keys[begin : begin + block], turned[h], NN)
                products = dot(values[begin : begin + block], turned[heads + h], NN)
                if masked:
                    scores = scores + mask[begin : begin + block]
                rows = scores.shape[1]
                scores = scores.reshape(-1, 8, rows)
                products = products.reshape(-1, 8, rows)
                raised = jnp.maximum(most_h, jnp.max(scores, axis=0))
                fade = jnp.exp2((most_h - raised) * factor)
                weights = jnp.exp2((scores - raised[None]) * factor)
                most_h = raised
                total_h = total_h * fade + jnp.sum(weights, axis=0)
                weighted_h = weighted_h * fade + jnp.sum(weights * products, axis=0)
            most[h], total[h], weighted[h] = most_h, total_h, weighted_h

    visit(0, True)

    @pl.loop(memory.shape[1] - info[0], memory.shape[1])
    def _(index):
        visit(index, False)

    for h in range(heads):
        top = jnp.max(most[h], axis=0, keepdims=True)
        fade = jnp.exp2((most[h] - top) * factor)
        out[0, h : h + 1] = top
        out[1, h : h + 1] = jnp.sum(total[h] * fade, axis=0, keepdims=True)
        out[2, h : h + 1] = jnp.sum(weighted[h] * fade, axis=0, keepdims=True)


def grads_kernel(
    heads, head, scale, info, own, other, memory, mine, theirs,
    own_grad, other_grad, memory_grad,
    mask, queries, grads, weights_half, slopes_half, query_grad, shift, delta,
):
    groups, block = memory.shape[0] // 2, 2 * memory.shape[2]
    half, rows = block // 2, 2 * block
    factor = scale * LOG2E
    fill_mask(info, mask, block, groups)

    def turned(stat):
        return jnp.concatenate([theirs[stat, :, block:], theirs[stat, :, :block]], axis=1)

    most = [mine[0], turned(0)]
    top = jnp.maximum(most[0], most[1])
    fades = [jnp.exp2((m - top) * factor) for m in most]
    total = mine[1] * fades[0] + turned(1) * fades[1]
    weighted = mine[2] * fades[0] + turned(2) * fades[1]
    shift[...] = top * factor + jnp.log(total) * LOG2E
    delta[...] = weighted / total
    for h in range(heads):
        queries[h * rows : (h + 1) * rows] = head_rows(own, other, h, head)
        grads[h * rows : (h + 1) * rows] = head_rows(own, other, heads + h, head)
    query_grad[...] = jnp.zeros(query_grad.shape, jnp.float32)

    def visit(index, masked):
        keys = group_of(memory, index, head, 0)
        values = group_of(memory, index, head, 1)
        for h in range(heads):
            cut = slice(h * rows, (h + 1) * rows)
            for begin in range(0, keys.shape[0], rows):
                part = slice(begin, begin + rows)
                scores = dot(keys[part], queries[cut], NT)
                products = dot(values[part], grads[cut], NT)
                if masked:
                    scores = scores + mask[part]
                weights = jnp.exp2(scores * factor - shift[h : h + 1])
                slopes = weights * (products - delta[h : h + 1])
                weights_half[part, cut] = weights.astype(jnp.bfloat16)
                slopes_half[part, cut] = slopes.astype(jnp.bfloat16)
        value_grad = dot(weights_half[...], grads[...], NN).astype(jnp.bfloat16)
        key_grad = (dot(slopes_half[...], queries[...], NN) * scale).astype(jnp.bfloat16)
        for g in range(2 * groups):
            cut = slice(g * half, (g + 1) * half)
            moved = jnp.logical_and(2 * index == memory.shape[1], info[0] == memory.shape[1] - 1)
            leaves = 2 * half_back(1, half_on(1, g // 2, groups), groups) + g % 2
            to = jnp.where(moved, leaves, g)
            memory_grad[to, index, :, :head] = key_grad[cut]
            memory_grad[to, index, :, head:] = value_grad[cut]
        query_grad[...] += dot(keys, slopes_half[...], TN)

    visit(0, True)

    @pl.loop(memory.shape[1] - info[0], memory.shape[1])
    def _(index):
        visit(index, False)

    for h in range(heads):
        piece = query_grad[:, h * rows : (h + 1) * rows].T * scale
        own_grad[:, h * head : (h + 1) * head] = piece[:block]
        other_grad[:, h * head : (h + 1) * head] = piece[block:].astype(jnp.bfloat16)


def track_kernel(heads, head, scale, span, queries, grads, memory, query_grad, memory_grad):
    tracks, positions, _ = memory.shape
    factor = scale * LOG2E
    key_place = lax.rem(lax.broadcasted_iota(jnp.int32, (tracks * span, heads * span), 0), span)
    row_place = lax.rem(lax.broadcasted_iota(jnp.int32, (tracks * span, heads * span), 1), span)
    mask = jnp.where(key_place == row_place, 0.0, FAR_BELOW)
    for begin in range(0, positions, span):
        at = slice(begin, begin + span)
        rows = jnp.concatenate([queries[at, h * head : (h + 1) * head] for h in range(heads)], axis=0)
        out_rows = jnp.concatenate([grads[at, h * head : (h + 1) * head] for h in range(heads)], axis=0)
        keys = jnp.concatenate([memory[t, at, :head] for t in range(tracks)], axis=0)
        values = jnp.concatenate([memory[t, at, head:] for t in range(tracks)], axis=0)
        scores = dot(keys, rows, NT) + mask
        products = dot(values, out_rows, NT)
        top = jnp.max(scores, axis=0, keepdims=True)
        raw = jnp.exp2((scores - top) * factor)
        inverse = 1.0 / jnp.sum(raw, axis=0, keepdims=True)
        weights = raw * inverse
        delta = jnp.sum(weights * products, axis=0, keepdims=True)
        slopes = weights * (products - delta)
        weights_half = weights.astype(jnp.bfloat16)
        slopes_half = slopes.astype(jnp.bfloat16)
        value_grad = dot(weights_half, out_rows, NN).astype(jnp.bfloat16)
        key_grad = (dot(slopes_half, rows, NN) * scale).astype(jnp.bfloat16)
        row_grad = (dot(keys, slopes_half, TN).T * scale).astype(jnp.bfloat16)
        for t in range(tracks):
            cut = slice(t * span, (t + 1) * span)
            memory_grad[t, at, :head] = key_grad[cut]
            memory_grad[t, at, head:] = value_grad[cut]
        for h in range(heads):
            query_grad[at, h * head : (h + 1) * head] = row_grad[h * span : (h + 1) * span]


def body(time_query, time_memory, time_grad_out, track_query, track_memory, track_grad_out):
    songs, pos_dev, _, feature = time_query.shape
    head = time_memory.shape[3] // 2
    heads = feature // head
    scale = head ** (-0.5)
    block = 2 * pos_dev
    rows = 2 * block
    core = lax.axis_index("core")
    side = lax.axis_index("side")
    low = lax.axis_index("low")
    high = lax.axis_index("high")
    n_low = lax.axis_size("low")
    n_high = lax.axis_size("high")
    tracks = lax.axis_size("track")
    info = jnp.stack([high, low, side, core]).astype(jnp.int32)

    def of_song(array, index):
        return lax.dynamic_index_in_dim(array, index, 0, keepdims=False)

    def places(step, half_ring):
        pairs = []
        for i in range(n_high - step):
            for j in range(n_low):
                to = half_ring(i, j, n_low) if 2 * step == n_high else j
                pairs.append((i * n_low + j, (i + step) * n_low + to))
        return pairs

    memory = time_memory[:, :, 0]
    with jax.named_scope("memory_high"):
        steps = range(n_high - 1, 0, -1)
        held = [memory] + [lax.ppermute(memory, ("high", "low"), places(s, half_on)) for s in steps]
    near = held[-1]
    with jax.named_scope("query_songs"):
        packed = jnp.concatenate([time_query[:, :, 0], time_grad_out[:, :, 0]], axis=2)
        packed = after(packed, held[1])
        own = jnp.concatenate(
            [of_song(packed, core), swapped(of_song(packed, 1 - core), "core")], axis=0
        )
    with jax.named_scope("query_sides"):
        other = swapped(own, "side")
    with jax.named_scope("memory_low"):
        everyone = jnp.stack([jnp.broadcast_to(h[None], (n_low, *h.shape)) for h in held], axis=2)
        held = lax.all_to_all(
            everyone.reshape(-1, *everyone.shape[2:]), ("low", "core"), 0, 0, tiled=True
        )
    bits = [1 << i for i in reversed(range((tracks - 1).bit_length()))]

    def across(array, bit):
        return lax.ppermute(array, "track", [(i, i ^ bit) for i in range(tracks)])

    with jax.named_scope("track_gather"):
        everything = after(track_memory.reshape(1, block, 2 * head), near)
        for bit in bits:
            everything = jnp.concatenate([everything, across(everything, bit)], axis=0)

    mine = pl.pallas_call(
        functools.partial(stats_kernel, heads, head, scale * LOG2E),
        out_shape=jax.ShapeDtypeStruct((3, heads, rows), jnp.float32),
        in_specs=[SMEM] + [VMEM] * 3,
        out_specs=VMEM,
        scratch_shapes=[
            pltpu.VMEM((n_low * block, rows), jnp.float32),
            pltpu.VMEM((2 * heads, head, rows), jnp.bfloat16),
        ]
        + [pltpu.VMEM((heads, 8, rows), jnp.float32)] * 3,
        compiler_params=PARAMS,
        name="time_stats",
    )(info, own, other, held)
    with jax.named_scope("stats_sides"):
        theirs = swapped(mine, "side")
    track_query_grad, track_partial = pl.pallas_call(
        functools.partial(track_kernel, heads, head, scale, 32),
        out_shape=(
            jax.ShapeDtypeStruct((block, feature), jnp.bfloat16),
            jax.ShapeDtypeStruct((tracks, block, 2 * head), jnp.bfloat16),
        ),
        in_specs=[VMEM] * 3,
        out_specs=(VMEM, VMEM),
        compiler_params=PARAMS,
        name="track_core",
    )(track_query.reshape(block, feature), track_grad_out.reshape(block, feature), after(everything, mine))
    theirs = after(theirs, track_partial)
    own_grad, other_grad, memory_grad = pl.pallas_call(
        functools.partial(grads_kernel, heads, head, scale),
        out_shape=(
            jax.ShapeDtypeStruct((block, feature), jnp.float32),
            jax.ShapeDtypeStruct((block, feature), jnp.bfloat16),
            jax.ShapeDtypeStruct((2 * n_low, n_high, pos_dev, 2 * head), jnp.bfloat16),
        ),
        in_specs=[SMEM] + [VMEM] * 5,
        out_specs=(VMEM, VMEM, VMEM),
        scratch_shapes=[
            pltpu.VMEM((n_low * block, rows), jnp.float32),
            pltpu.VMEM((heads * rows, head), jnp.bfloat16),
            pltpu.VMEM((heads * rows, head), jnp.bfloat16),
            pltpu.VMEM((n_low * block, heads * rows), jnp.bfloat16),
            pltpu.VMEM((n_low * block, heads * rows), jnp.bfloat16),
            pltpu.VMEM((head, heads * rows), jnp.float32),
            pltpu.VMEM((heads, rows), jnp.float32),
            pltpu.VMEM((heads, rows), jnp.float32),
        ],
        compiler_params=PARAMS,
        name="time_grads",
    )(info, own, other, held, mine, theirs)

    with jax.named_scope("memory_grad_low"):
        parts = lax.all_to_all(memory_grad, ("low", "core"), 0, 0, tiled=True)
        parts = parts.reshape(n_low, 2, n_high, pos_dev, 2 * head)
        sums = jnp.sum(parts.astype(jnp.float32), axis=0)
    with jax.named_scope("memory_grad_high"):
        gathered = sums[:, 0]
        for s in (3, 2, 1):
            came = lax.ppermute(
                sums[:, n_high - s].astype(jnp.bfloat16),
                ("high", "low"),
                [(to, origin) for origin, to in places(s, half_back)],
            )
            gathered = gathered + came.astype(jnp.float32)
        time_memory_grad = gathered.astype(jnp.bfloat16).reshape(time_memory.shape)

    def to_songs(array):
        ours = array[:pos_dev]
        back = swapped(array[pos_dev:], "core")
        first = jnp.where(core == 0, ours, back)
        second = jnp.where(core == 0, back, ours)
        return jnp.stack([first, second])[:, :, None, :]

    with jax.named_scope("query_grad_sides"):
        query_grad = own_grad + swapped(other_grad, "side").astype(jnp.float32)
    with jax.named_scope("query_grad_songs"):
        time_query_grad = to_songs(query_grad.astype(jnp.bfloat16))
    with jax.named_scope("track_scatter"):
        partial = track_partial
        for bit in reversed(bits):
            kept, sent = jnp.split(partial, 2)
            back = across(sent.astype(jnp.bfloat16), bit)
            partial = kept.astype(jnp.float32) + back.astype(jnp.float32)
        track_memory_grad = partial.astype(jnp.bfloat16)
    return (
        time_query_grad,
        time_memory_grad,
        track_query_grad.reshape(track_query.shape),
        track_memory_grad.reshape(track_memory.shape),
    )


def solution(mesh):
    tracks, times = mesh.devices.shape
    chips = times // 4
    high = next(n for n in (4, 2, 1) if chips % n == 0)
    axes = ("track", "high", "low", "side", "core")
    finer = Mesh(mesh.devices.reshape(tracks, high, chips // high, 2, 2), axes)
    placed = P(None, axes[1:], "track", None)
    return jax.shard_map(
        body,
        mesh=finer,
        in_specs=(placed,) * 6,
        out_specs=(placed,) * 4,
        check_vma=False,
    )
```
